32 devices in a mesh: svc: 8 (over z, x), step: 4 (over y, core).
Axes of the slice: x: 2, y: 2, z: 4, core: 2. Of those that a mesh axis runs over, the one named last changes fastest.
Arguments:
- service_factors: bfloat16 [49152, 256], P('svc'), may hold values from -1.5 to 1.5
- step_factors: bfloat16 [4096, 256], P('step'), may hold values from -1.5 to 1.5
- block_rows: int32 [8, 4, 154], P('svc', 'step'), may hold values from 0 to 47, as said below
- block_cols: int32 [8, 4, 154], P('svc', 'step'), may hold values from 0 to 7
- block_counts: int32 [8, 4], P('svc', 'step'), may hold values from 1 to 154, as said below
- block_values: bfloat16 [8, 4, 154, 128, 128], P('svc', 'step'), may hold values from -6 to 6
Outputs:
- new_services: bfloat16 [49152, 256], P('svc')
- new_steps: bfloat16 [4096, 256], P('step')
The draws below stay inside these ranges and needn't reach their ends.
Inputs may be any that keep to these rules, and one draw needn't show every extreme that they name: Within one tile's 154 slots the pairs (block_rows, block_cols) are all different. `block_counts`: some tile has all 154 slots observed.
All inputs are finite; a program needn't handle non-finite values.
Results may differ from the reference program's by a relative error of at most 0.002.
The reference program's roundings to bfloat16 on the way count: a program that leaves them out, or rounds other values in their place, can miss the bound.
Values may be sent and summed in bfloat16 or wider, within the bound.
No kernel may reach another device: no remote copies, remote signals or barrier semaphores. Data moves between devices by JAX's collectives and lax.ppermute only.
A program may use at most 128 MiB of HBM per device.

```python
import jax
import jax.numpy as jnp
from jax import lax

R = 256
SB = 48
TB = 8
NB_MAX = 154
SERVICES = 49152
STEPS = 4096
N_SVC = 8
N_STEP = 4


def block_order(key):
    subkeys = jax.random.split(jax.random.fold_in(key, 11), N_SVC * N_STEP)

    def one_tile(subkey):
        return jax.random.permutation(subkey, SB * TB)[:NB_MAX]
    orders = jax.vmap(one_tile)(subkeys)
    return orders.reshape(N_SVC, N_STEP, NB_MAX).astype(jnp.int32)


def draw_block_rows(key, part):
    return block_order(key) // TB


def draw_block_cols(key, part):
    return block_order(key) % TB


def draw_block_counts(key, part):
    first_key, second_key = jax.random.split(jax.random.fold_in(key, 23))
    counts = jax.random.randint(first_key, (N_SVC * N_STEP,), 1, NB_MAX + 1)
    full_tile = jax.random.randint(second_key, (), 0, N_SVC * N_STEP)
    counts = jnp.where(jnp.arange(N_SVC * N_STEP) == full_tile, NB_MAX, counts)
    return counts.reshape(N_SVC, N_STEP).astype(jnp.int32)


def block_scale(stream_key, dims, cuts, smallest, high):
    gain, own = 1.0, jax.random.fold_in(stream_key, 6)
    for axis_at, parts in cuts:
        steps = jnp.exp(jax.random.uniform(jax.random.fold_in(own, axis_at), (parts,), jnp.float32, smallest / len(cuts), high / len(cuts)))
        gain = gain * jnp.repeat(steps, dims[axis_at] // parts).reshape([-1 if axis == axis_at else 1 for axis in range(len(dims))])
    return gain


def gaussian(own_key, shape, spread, limit, shards=(), kind=jnp.bfloat16):
    drawn = spread * jax.random.normal(own_key, shape, jnp.float32)
    if shards:
        drawn = drawn * block_scale(own_key, shape, shards, -0.22, 0.18)
    return jnp.clip(drawn, -limit, limit).astype(kind)


def setup_inputs(seed: int = 0) -> dict:
    key_list = jax.random.split(jax.random.key(seed), 7)
    return {
        "service_factors": gaussian(key_list[0], (SERVICES, R), 0.25, 1.5, ((0, 8),)),
        "step_factors": gaussian(key_list[1], (STEPS, R), 0.25, 1.5, ((0, 4),)),
        "block_rows": draw_block_rows(jax.random.fold_in(key_list[6], 71), 0),
        "block_cols": draw_block_cols(jax.random.fold_in(key_list[6], 71), 0),
        "block_counts": draw_block_counts(jax.random.fold_in(key_list[6], 71), 0),
        "block_values": gaussian(key_list[5], (N_SVC, N_STEP, NB_MAX, 128, 128), 1.0, 6.0, ((0, 8), (1, 4))),
    }


step_u = 0.03
step_v = 0.02
ridge = 0.1
smooth = 20.0


def reference(service_factors, step_factors, block_rows, block_cols, block_counts, block_values):
    tile_total = N_SVC * N_STEP
    u_tiles = service_factors.reshape(SERVICES // 128, 128, R)
    v_tiles = step_factors.reshape(STEPS // 128, 128, R)
    row_lists = block_rows.reshape(tile_total, NB_MAX)
    col_lists = block_cols.reshape(tile_total, NB_MAX)
    count_list = block_counts.reshape(tile_total)
    value_list = block_values.reshape(tile_total, NB_MAX, 128, 128)
    tile_ids = jnp.arange(tile_total, dtype=jnp.int32)
    slot_ids = jnp.arange(NB_MAX, dtype=jnp.int32)

    def locate(tile_id, row_list, col_list):
        global_rows = (tile_id // N_STEP) * SB + row_list
        global_cols = (tile_id % N_STEP) * TB + col_list
        return global_rows.astype(jnp.int32), global_cols.astype(jnp.int32)

    def residual(left_blocks, right_blocks, values, count):
        predicted = jnp.einsum("nir,njr->nij", left_blocks.astype(jnp.float32), right_blocks.astype(jnp.float32))
        live_mask = (slot_ids < count).astype(jnp.float32)
        return ((predicted - values.astype(jnp.float32)) * live_mask[:, None, None]).astype(jnp.bfloat16)

    def u_pass(total, item):
        tile_id, row_list, col_list, count, values = item
        global_rows, global_cols = locate(tile_id, row_list, col_list)
        right_blocks = v_tiles[global_cols]
        errors = residual(u_tiles[global_rows], right_blocks, values, count)
        grads = jnp.einsum("nij,njr->nir", errors.astype(jnp.float32), right_blocks.astype(jnp.float32))
        return total.at[global_rows].add(grads), None

    grad_u, _ = lax.scan(u_pass, jnp.zeros((SERVICES // 128, 128, R), jnp.float32),
                         (tile_ids, row_lists, col_lists, count_list, value_list))
    old_u = service_factors.astype(jnp.float32)
    new_services = (old_u - step_u * (grad_u.reshape(SERVICES, R) + ridge * old_u)).astype(jnp.bfloat16)
    new_tiles = new_services.reshape(SERVICES // 128, 128, R)

    def v_pass(total, item):
        tile_id, row_list, col_list, count, values = item
        global_rows, global_cols = locate(tile_id, row_list, col_list)
        left_blocks = new_tiles[global_rows]
        errors = residual(left_blocks, v_tiles[global_cols], values, count)
        grads = jnp.einsum("nij,nir->njr", errors.astype(jnp.float32), left_blocks.astype(jnp.float32))
        return total.at[global_cols].add(grads), None

    grad_v, _ = lax.scan(v_pass, jnp.zeros((STEPS // 128, 128, R), jnp.float32),
                         (tile_ids, row_lists, col_lists, count_list, value_list))
    old_v = step_factors.astype(jnp.float32)
    laplace = 2.0 * old_v - jnp.roll(old_v, 1, 0) - jnp.roll(old_v, -1, 0)
    new_steps = (old_v - step_v * (grad_v.reshape(STEPS, R) + ridge * old_v + smooth * laplace)).astype(jnp.bfloat16)
    return new_services, new_steps
```

```python
import functools

import jax
import jax.numpy as jnp
from jax import lax
from jax.experimental import pallas as pl
from jax.experimental.pallas import tpu as pltpu
from jax.sharding import PartitionSpec as P

step_u = 0.03
step_v = 0.02
ridge = 0.1
smooth = 20.0

f32, bf16, i32, i16 = jnp.float32, jnp.bfloat16, jnp.int32, jnp.int16
B = 128
PAD = 16
TOP = 32000.0
ROWS_BY_ROWS = (((1,), (1,)), ((), ()))
COLS_BY_COLS = (((0,), (0,)), ((), ()))

SMEM = pl.BlockSpec(memory_space=pltpu.SMEM)
VMEM = pl.BlockSpec(memory_space=pltpu.VMEM)
ANY = pl.BlockSpec(memory_space=pl.ANY)


def params():
    return pltpu.CompilerParams(vmem_limit_bytes=40 * 2**20)


def encode(x):
    rows, width = x.shape
    group = min(rows, B)
    line = lax.broadcasted_iota(i32, (PAD, width), 0)
    powers = jnp.zeros((PAD, width), f32)
    parts = []
    for g in range(rows // group):
        part = x[g * group : (g + 1) * group]
        top = jnp.max(jnp.abs(part), axis=0, keepdims=True)
        power = jnp.ceil(jnp.log2(jnp.maximum(top, 1e-30)))
        parts.append(jnp.round(part * (jnp.exp2(-power) * TOP)))
        powers = jnp.where(line == g, power, powers)
    return [p.astype(i32).astype(i16) for p in parts], powers.astype(i32).astype(i16)


def store_code(ref, x):
    parts, powers = encode(x)
    group = parts[0].shape[0]
    for g, part in enumerate(parts):
        ref[g * group : (g + 1) * group, :] = part
    ref[x.shape[0] :, :] = powers


def decode(ref, g, group):
    rows = ref.shape[0] - PAD
    powers = ref[rows:, :].astype(i32).astype(f32)[g : g + 1]
    return ref[g * group : (g + 1) * group, :].astype(i32).astype(f32) * (
        jnp.exp2(powers) * (1.0 / TOP)
    )


def fetch(slots, values, dense, sem, first, count, across):
    def go(i, started):
        slot = slots[first * across + i]

        @pl.when(slot >= 0)
        def _():
            row = pl.multiple_of((i // across) * B, B)
            pltpu.make_async_copy(
                values.at[slot], dense.at[lax.rem(i, across), pl.ds(row, B)], sem
            ).start()

        return started + (slot >= 0).astype(i32)

    return lax.fori_loop(0, count * across, go, jnp.int32(0), unroll=across)


def drain(started, values, dense, sem):
    def wait(_, c):
        pltpu.make_async_copy(values.at[0], dense.at[0, pl.ds(0, B)], sem).wait()
        return c

    lax.fori_loop(0, started, wait, 0)


def residual(left, v_ref, dense, err, slots, first, count, across):
    wide = min(2, across)
    for t in range(0, across, wide):
        predicted = lax.dot_general(
            left, v_ref[t * B : (t + wide) * B, :], ROWS_BY_ROWS, preferred_element_type=f32
        )
        for r in range(count):
            rows = slice(r * B, (r + 1) * B)
            for c in range(t, t + wide):
                live = slots[(first + r) * across + c] >= 0
                gap = predicted[rows, (c - t) * B : (c - t + 1) * B] - dense[c, rows, :].astype(f32)
                err[rows, c * B : (c + 1) * B] = jnp.where(live, gap, 0.0).astype(bf16)


def u_body(first, count, down, across, opening, *refs):
    if opening:
        row_ref, col_ref, live_ref, u_hbm, v_ref, values, out, slots, dense, err, left, sem, usem = refs
    else:
        slots, u_hbm, v_ref, values, out, dense, err, left, sem, usem = refs
    load = pltpu.make_async_copy(u_hbm.at[pl.ds(first * B, count * B)], left, usem)
    load.start()
    if opening:

        def clear(i, c):
            slots[i] = jnp.int32(-1)
            return c

        lax.fori_loop(0, down * across, clear, 0, unroll=8)

        def enter(k, c):
            slots[row_ref[k] * across + col_ref[k]] = k
            return c

        lax.fori_loop(0, live_ref[0], enter, 0)
    started = fetch(slots, values, dense, sem, first, count, across)
    load.wait()
    drain(started, values, dense, sem)
    residual(left[...], v_ref, dense, err, slots, first, count, across)
    out[...] = jnp.dot(err[...], v_ref[...], preferred_element_type=f32)


def work_scratch(count, across, width):
    return [
        pltpu.VMEM((across, count * B, B), bf16),
        pltpu.VMEM((count * B, across * B), bf16),
        pltpu.VMEM((count * B, width), bf16),
        pltpu.SemaphoreType.DMA,
        pltpu.SemaphoreType.DMA,
    ]


def u_pass(first, count, down, across, width, index, u, v, values):
    opening = isinstance(index, tuple)
    out = [jax.ShapeDtypeStruct((count * B, width), f32)]
    out_specs = [VMEM]
    if opening:
        out.append(jax.ShapeDtypeStruct((down * across,), i32))
        out_specs.append(SMEM)
    ins = list(index) if opening else [index]
    return pl.pallas_call(
        functools.partial(u_body, first, count, down, across, opening),
        out_shape=out,
        in_specs=[SMEM] * len(ins) + [ANY, VMEM, ANY],
        out_specs=out_specs,
        scratch_shapes=work_scratch(count, across, width),
        compiler_params=params(),
        cost_estimate=pl.CostEstimate(
            flops=4 * count * B * across * B * width, bytes_accessed=count * B * width * 6, transcendentals=0
        ),
        name=f"u_pass_{first}",
    )(*ins, u, v, values)


def sum_body(place, own, other, mine_out, rest_out):
    half = own.shape[0] // 2
    core = place[0]
    for out, at in ((mine_out, core), (rest_out, 1 - core)):
        rows = pl.ds(pl.multiple_of(at * half, 8), half)
        store_code(out, own[rows, :] + other[rows, :])


def chip_sum(place, own, other):
    rows, width = own.shape
    code = jax.ShapeDtypeStruct((rows // 2 + PAD, width), i16)
    return pl.pallas_call(
        sum_body,
        out_shape=[code, code],
        in_specs=[SMEM, VMEM, VMEM],
        out_specs=[VMEM, VMEM],
        compiler_params=params(),
        cost_estimate=pl.CostEstimate(flops=rows * width * 8, bytes_accessed=rows * width * 10, transcendentals=0),
        name="chip_sum",
    )(place, own, other)


def again_body(mine, rest, mine_in, rest_in, mine_out, rest_out):
    rows = mine.shape[0] - PAD
    group = min(rows, B)
    for out, a, b in ((mine_out, mine, mine_in), (rest_out, rest, rest_in)):
        whole = [decode(a, g, group) + decode(b, g, group) for g in range(rows // group)]
        store_code(out, jnp.concatenate(whole, axis=0))


def chip_sum_again(*codes):
    code = jax.ShapeDtypeStruct(codes[0].shape, i16)
    return pl.pallas_call(
        again_body,
        out_shape=[code, code],
        in_specs=[VMEM] * 4,
        out_specs=[VMEM, VMEM],
        compiler_params=params(),
        name="chip_sum_again",
    )(*codes)


def v_body(first, count, across, opening, shards, *refs):
    slots, place, u_hbm, v_ref, values, mine, rest, mine_in, rest_in = refs[:9]
    refs = refs[9:]
    if not opening:
        before, _ = refs[:2]
        refs = refs[2:]
    new_out, refs = refs[0], refs[1:]
    if shards:
        own_out, sent, refs = refs[0], refs[1:shards], refs[shards:]
    else:
        total, refs = refs[0], refs[1:]
    dense, err, left, sem, usem = refs[:5]
    load = pltpu.make_async_copy(u_hbm.at[pl.ds(first * B, count * B)], left, usem)
    load.start()
    started = fetch(slots, values, dense, sem, first, count, across)
    load.wait()
    half = count * B // 2
    group = min(half, B)
    for a, b, at in ((mine, mine_in, place[0]), (rest, rest_in, 1 - place[0])):
        for g in range(half // group):
            rows = pl.ds(pl.multiple_of(at * half + g * group, 16), group)
            old = left[rows, :].astype(f32)
            grad = decode(a, g, group) + decode(b, g, group)
            left[rows, :] = (old - step_u * (grad + ridge * old)).astype(bf16)
    save = pltpu.make_async_copy(left, new_out.at[pl.ds(first * B, count * B)], usem)
    save.start()
    drain(started, values, dense, sem)
    residual(left[...], v_ref, dense, err, slots, first, count, across)
    part = lax.dot_general(left[...], err[...], COLS_BY_COLS, preferred_element_type=f32)
    if not opening:
        part = part + before[...]
    if not shards:
        total[...] = part
    else:
        turned = refs[5]
        turned[...] = part.T
        rows = turned.shape[0] // shards
        here = place[1]
        own_out[...] = turned[pl.ds(pl.multiple_of(here * rows, 8), rows), :]
        for d in range(1, shards):
            there = jnp.bitwise_xor(here, d)
            store_code(sent[d - 1], turned[pl.ds(pl.multiple_of(there * rows, 8), rows), :])
    save.wait()


def v_pass(first, count, across, slots, place, u, v, values, codes, before, shards):
    width = u.shape[1]
    times = v.shape[0]
    opening = before is None
    ins = [slots, place, u, v, values, *codes]
    in_specs = [SMEM, SMEM, ANY, VMEM, ANY] + [VMEM] * 4
    aliases = {}
    out = [jax.ShapeDtypeStruct(u.shape, bf16)]
    out_specs = [ANY]
    if not opening:
        ins += [before[1], before[0]]
        in_specs += [VMEM, ANY]
        aliases = {10: 0}
    scratch = work_scratch(count, across, width)
    if shards:
        rows = times // shards
        out.append(jax.ShapeDtypeStruct((rows, width), f32))
        out += [jax.ShapeDtypeStruct((rows + PAD, width), i16)] * (shards - 1)
        out_specs += [VMEM] * shards
        scratch.append(pltpu.VMEM((times, width), f32))
    else:
        out.append(jax.ShapeDtypeStruct((width, times), f32))
        out_specs.append(VMEM)
    return pl.pallas_call(
        functools.partial(v_body, first, count, across, opening, shards),
        out_shape=out,
        in_specs=in_specs,
        out_specs=out_specs,
        input_output_aliases=aliases,
        scratch_shapes=scratch,
        compiler_params=params(),
        cost_estimate=pl.CostEstimate(
            flops=4 * count * B * across * B * width, bytes_accessed=count * B * width * 6, transcendentals=0
        ),
        name=f"v_pass_{first}",
    )(*ins)


def last_body(place, v_ref, low, high, own, *refs):
    codes, out, wide = refs[:-2], refs[-2], refs[-1]
    times = v_ref.shape[0]
    rows = out.shape[0]
    group = min(rows, B)
    wide[:PAD, :] = low[...]
    wide[PAD : PAD + times, :] = v_ref[...]
    wide[PAD + times :, :] = high[...]
    start = pl.multiple_of(place[1] * rows, 16)
    window = wide[pl.ds(start, rows + 2 * PAD), :].astype(f32)
    old = window[PAD : PAD + rows]
    lap = 2.0 * old - window[PAD - 1 : PAD - 1 + rows] - window[PAD + 1 : PAD + 1 + rows]
    for g in range(rows // group):
        at = slice(g * group, (g + 1) * group)
        grad = own[at, :]
        for code in codes:
            grad = grad + decode(code, g, group)
        out[at, :] = (old[at] - step_v * (grad + ridge * old[at] + smooth * lap[at])).astype(bf16)


def last_step(place, v, low, high, own, codes):
    return pl.pallas_call(
        last_body,
        out_shape=jax.ShapeDtypeStruct(own.shape, bf16),
        in_specs=[SMEM] + [VMEM] * (4 + len(codes)),
        out_specs=VMEM,
        scratch_shapes=[pltpu.VMEM((v.shape[0] + 2 * PAD, v.shape[1]), bf16)],
        compiler_params=params(),
        name="last_step",
    )(place, v, low, high, own, *codes)


def join_body(place, *refs):
    out = refs[-1]
    rows = refs[0].shape[0]
    for d, part in enumerate(refs[:-1]):
        there = jnp.bitwise_xor(place[1], d)
        out[pl.ds(pl.multiple_of(there * rows, 16), rows), :] = part[...]


def join(place, parts):
    rows, width = parts[0].shape
    return pl.pallas_call(
        join_body,
        out_shape=jax.ShapeDtypeStruct((rows * len(parts), width), bf16),
        in_specs=[SMEM] + [VMEM] * len(parts),
        out_specs=VMEM,
        compiler_params=params(),
        name="join",
    )(place, *parts)


def swap(x, axis, mask):
    return lax.ppermute(x, axis, [(i, i ^ mask) for i in range(lax.axis_size(axis))])


def shift(x, axis, by):
    n = lax.axis_size(axis)
    return lax.ppermute(x, axis, [(i, (i + by) % n) for i in range(n)])


def chunks_of(down):
    unit = down // 8
    sizes = [unit, 2 * unit, 2 * unit, 2 * unit]
    sizes.append(down - sum(sizes))
    return [(sum(sizes[:i]), size) for i, size in enumerate(sizes)]


def on_device(u, v, block_rows, block_cols, block_counts, block_values):
    width = u.shape[1]
    down, across = u.shape[0] // B, v.shape[0] // B
    values = block_values[0, 0]
    steps, peers = lax.axis_size("step"), lax.axis_size("svc")
    place = jnp.stack([lax.axis_index("step") % 2, lax.axis_index("svc")]).astype(i32)
    low = shift(v[-PAD:], "step", 1)
    high = shift(v[:PAD], "step", -1)
    chunks = chunks_of(down)
    index = (block_rows[0, 0], block_cols[0, 0], block_counts[0])
    codes = []
    for first, count in chunks:
        got = u_pass(first, count, down, across, width, index, u, v, values)
        if first == 0:
            index = got[1]
        mine, rest = chip_sum(place, got[0], swap(got[0], "step", 1))
        mask = 2
        while True:
            mine_in = swap(mine, "step", mask)
            rest_in = swap(mine_in, "step", 1)
            mask *= 2
            if mask >= steps:
                break
            mine, rest = chip_sum_again(mine, rest, mine_in, rest_in)
        codes.append((mine, rest, mine_in, rest_in))
    before = None
    for i, (first, count) in enumerate(chunks):
        shards = peers if i == len(chunks) - 1 else 0
        before = v_pass(first, count, across, index, place, u, v, values, codes[i], before, shards)
    new_services, own, sent = before[0], before[1], before[2:]
    arrived = [swap(x, "svc", d + 1) for d, x in enumerate(sent)]
    part = last_step(place, v, low, high, own, arrived)
    parts = [part] + [swap(part, "svc", d) for d in range(1, peers)]
    return new_services, join(place, parts)


def solution(mesh):
    return jax.shard_map(
        on_device,
        mesh=mesh,
        in_specs=(
            P("svc", None),
            P("step", None),
            P("svc", "step", None),
            P("svc", "step", None),
            P("svc", "step"),
            P("svc", "step", None, None, None),
        ),
        out_specs=(P("svc", None), P("step", None)),
        check_vma=False,
    )
```

```python
import functools

import jax
import jax.numpy as jnp
from jax import lax
from jax.experimental import pallas as pl
from jax.experimental.pallas import tpu as pltpu
from jax.sharding import PartitionSpec as P

step_u = 0.03
step_v = 0.02
ridge = 0.1
smooth = 20.0

f32, bf16, i32, i16 = jnp.float32, jnp.bfloat16, jnp.int32, jnp.int16
B = 128
PAD = 16
TOP = 32000.0
ROWS_BY_ROWS = (((1,), (1,)), ((), ()))
COLS_BY_COLS = (((0,), (0,)), ((), ()))

SMEM = pl.BlockSpec(memory_space=pltpu.SMEM)
VMEM = pl.BlockSpec(memory_space=pltpu.VMEM)
ANY = pl.BlockSpec(memory_space=pl.ANY)


SMALL = pl.CostEstimate(flops=1, bytes_accessed=1, transcendentals=0)


def params():
    return pltpu.CompilerParams(vmem_limit_bytes=24 * 2**20)


def encode(x):
    rows, width = x.shape
    group = min(rows, B)
    line = lax.broadcasted_iota(i32, (PAD, width), 0)
    powers = jnp.zeros((PAD, width), f32)
    parts = []
    for g in range(rows // group):
        part = x[g * group : (g + 1) * group]
        top = jnp.max(jnp.abs(part), axis=0, keepdims=True)
        power = jnp.ceil(jnp.log2(jnp.maximum(top, 1e-30)))
        parts.append(jnp.round(part * (jnp.exp2(-power) * TOP)))
        powers = jnp.where(line == g, power, powers)
    return [p.astype(i32).astype(i16) for p in parts], powers.astype(i32).astype(i16)


def store_code(ref, x):
    parts, powers = encode(x)
    group = parts[0].shape[0]
    for g, part in enumerate(parts):
        ref[g * group : (g + 1) * group, :] = part
    ref[x.shape[0] :, :] = powers


def decode(ref, g, group):
    rows = ref.shape[0] - PAD
    powers = ref[rows:, :].astype(i32).astype(f32)[g : g + 1]
    return ref[g * group : (g + 1) * group, :].astype(i32).astype(f32) * (
        jnp.exp2(powers) * (1.0 / TOP)
    )


def my_core():
    return lax.rem(lax.axis_index("step"), 2)


def two_halves(rows):
    half = rows // 2
    core = my_core()
    return [pl.ds(pl.multiple_of(at * half, 16), half) for at in (core, 1 - core)]


def residual(left, v_ref, block, err, slots, first, count, across):
    wide = min(2, across)
    for t in range(0, across, wide):
        predicted = lax.dot_general(
            left, v_ref[t * B : (t + wide) * B, :], ROWS_BY_ROWS, preferred_element_type=f32
        )
        for r in range(count):
            rows = slice(r * B, (r + 1) * B)
            for c in range(t, t + wide):
                slot = slots[(first + r) * across + c]
                gap = predicted[rows, (c - t) * B : (c - t + 1) * B] - block(slot, r, c).astype(f32)
                err[rows, c * B : (c + 1) * B] = jnp.where(slot >= 0, gap, 0.0).astype(bf16)


def split_product(err, v_ref, outs):
    for out, rows in zip(outs, two_halves(err.shape[0])):
        out[...] = jnp.dot(err[rows, :], v_ref[...], preferred_element_type=f32)


def first_u_body(
    count, down, across, row_hbm, col_hbm, live_hbm, u_hbm, v_hbm, values,
    keep, send, slots, row_ref, col_ref, live_ref, dense, err, left, v_ref, sems
):
    loads = [
        pltpu.make_async_copy(src, dst, sems.at[i])
        for i, (src, dst) in enumerate(
            (
                (row_hbm, row_ref),
                (col_hbm, col_ref),
                (live_hbm, live_ref),
                (u_hbm.at[pl.ds(0, count * B)], left),
                (v_hbm, v_ref),
            )
        )
    ]
    for load in loads:
        load.start()

    def clear(i, c):
        slots[i] = jnp.int32(-1)
        return c

    lax.fori_loop(0, down * across, clear, 0, unroll=8)
    for load in loads[:3]:
        load.wait()
    live = live_ref[0, 0]

    def enter(k, c):
        slots[row_ref[0, 0, k] * across + col_ref[0, 0, k]] = jnp.where(k < live, k, -1)
        return c

    lax.fori_loop(0, row_ref.shape[2], enter, 0, unroll=7)
    sem = sems.at[len(loads)]

    def fetch(i, started):
        slot = slots[i]

        @pl.when(slot >= 0)
        def _():
            row = pl.multiple_of((i // across) * B, B)
            pltpu.make_async_copy(
                values.at[slot], dense.at[lax.rem(i, across), pl.ds(row, B)], sem
            ).start()

        return started + (slot >= 0).astype(i32)

    started = lax.fori_loop(0, count * across, fetch, jnp.int32(0), unroll=across)
    for load in loads[3:]:
        load.wait()

    def wait(_, c):
        pltpu.make_async_copy(values.at[0], dense.at[0, pl.ds(0, B)], sem).wait()
        return c

    lax.fori_loop(0, started, wait, 0)
    block = lambda slot, r, c: dense[c, r * B : (r + 1) * B, :]
    residual(left[...], v_ref, block, err, slots, 0, count, across)
    split_product(err, v_ref, (keep, send))


def in_hbm(x):
    return pltpu.with_memory_space_constraint(x, pltpu.HBM)


def first_u_pass(count, down, across, index, u, v, values):
    rows, width = count * B, u.shape[1]
    hbm = pl.BlockSpec(memory_space=pltpu.HBM)
    part = jax.ShapeDtypeStruct((rows // 2, width), f32)
    return pl.pallas_call(
        functools.partial(first_u_body, count, down, across),
        out_shape=[part, part, jax.ShapeDtypeStruct((down * across,), i32)],
        in_specs=[hbm, hbm, ANY, hbm, hbm, hbm],
        out_specs=[VMEM, VMEM, SMEM],
        scratch_shapes=[
            *(pltpu.SMEM(x.shape, i32) for x in index),
            pltpu.VMEM((across, rows, B), bf16),
            pltpu.VMEM((rows, across * B), bf16),
            pltpu.VMEM((rows, width), bf16),
            pltpu.VMEM(v.shape, bf16),
            pltpu.SemaphoreType.DMA((6,)),
        ],
        compiler_params=params(),
        cost_estimate=SMALL,
        name="u_pass_0",
    )(*(in_hbm(x) for x in index[:2]), index[2], *(in_hbm(x) for x in (u, v, values)))


def u_body(first, count, across, waits, slots, u_ref, v_ref, values, *refs):
    keep, send, err = refs[waits:]
    block = lambda slot, r, c: values[jnp.maximum(slot, 0)]
    residual(u_ref[first * B : (first + count) * B, :], v_ref, block, err, slots, first, count, across)
    split_product(err, v_ref, (keep, send))


def u_pass(first, count, across, slots, u, v, values, after):
    rows, width = count * B, u.shape[1]
    part = jax.ShapeDtypeStruct((rows // 2, width), f32)
    return pl.pallas_call(
        functools.partial(u_body, first, count, across, len(after)),
        out_shape=[part, part],
        in_specs=[SMEM, VMEM, VMEM, VMEM] + [ANY] * len(after),
        out_specs=[VMEM, VMEM],
        scratch_shapes=[pltpu.VMEM((rows, across * B), bf16)],
        compiler_params=params(),
        cost_estimate=SMALL,
        name=f"u_pass_{first}",
    )(slots, u, v, values, *after)


def sum_body(own, other, *refs):
    store_code(refs[-1], own[...] + other[...])


def core_sum(own, other, after):
    rows, width = own.shape
    return pl.pallas_call(
        sum_body,
        out_shape=jax.ShapeDtypeStruct((rows + PAD, width), i16),
        in_specs=[VMEM, VMEM] + [ANY] * len(after),
        out_specs=VMEM,
        compiler_params=params(),
        cost_estimate=SMALL,
        name="core_sum",
    )(own, other, *after)


def again_body(mine, mine_in, out):
    rows = mine.shape[0] - PAD
    group = min(rows, B)
    whole = [decode(mine, g, group) + decode(mine_in, g, group) for g in range(rows // group)]
    store_code(out, jnp.concatenate(whole, axis=0))


def chip_sum(code, code_in):
    return pl.pallas_call(
        again_body,
        out_shape=jax.ShapeDtypeStruct(code.shape, i16),
        in_specs=[VMEM, VMEM],
        out_specs=VMEM,
        compiler_params=params(),
        name="chip_sum",
    )(code, code_in)


def update_body(first, code, code_in, u_ref, *refs):
    out = refs[-1]
    half = out.shape[0]
    group = min(half, B)
    start = first * B + my_core() * half
    for g in range(half // group):
        old = u_ref[pl.ds(pl.multiple_of(start + g * group, 16), group), :].astype(f32)
        grad = decode(code, g, group) + decode(code_in, g, group)
        out[g * group : (g + 1) * group, :] = (old - step_u * (grad + ridge * old)).astype(bf16)


def update(first, code, code_in, u, after):
    rows, width = code.shape[0] - PAD, code.shape[1]
    return pl.pallas_call(
        functools.partial(update_body, first),
        out_shape=jax.ShapeDtypeStruct((rows, width), bf16),
        in_specs=[VMEM, VMEM, VMEM] + [ANY] * len(after),
        out_specs=VMEM,
        compiler_params=params(),
        cost_estimate=SMALL,
        name=f"update_{first}",
    )(code, code_in, u, *after)


def v_body(first, count, across, opening, shards, *refs):
    slots, v_ref, values, own, other = refs[:5]
    refs = refs[5:]
    if not opening:
        before = refs[0]
        refs = refs[2:]
    new_out, refs = refs[0], refs[1:]
    if shards:
        own_out, sent, refs = refs[0], refs[1:shards], refs[shards:]
    else:
        total, refs = refs[0], refs[1:]
    err, left, sem = refs[:3]
    for src, rows in zip((own, other), two_halves(count * B)):
        left[rows, :] = src[...]
    save = pltpu.make_async_copy(left, new_out.at[pl.ds(first * B, count * B)], sem)
    save.start()
    block = lambda slot, r, c: values[jnp.maximum(slot, 0)]
    residual(left[...], v_ref, block, err, slots, first, count, across)
    part = lax.dot_general(left[...], err[...], COLS_BY_COLS, preferred_element_type=f32)
    if not opening:
        part = part + before[...]
    if not shards:
        total[...] = part
    else:
        turned = refs[3]
        turned[...] = part.T
        rows = turned.shape[0] // shards
        here = lax.axis_index("svc")
        own_out[...] = turned[pl.ds(pl.multiple_of(here * rows, 8), rows), :]
        for d in range(1, shards):
            there = jnp.bitwise_xor(here, d)
            store_code(sent[d - 1], turned[pl.ds(pl.multiple_of(there * rows, 8), rows), :])
    save.wait()


def v_pass(first, count, across, slots, shape, v, values, halves, before, shards):
    width = v.shape[1]
    times = v.shape[0]
    opening = before is None
    ins = [slots, v, values, *halves]
    in_specs = [SMEM] + [VMEM] * 4
    aliases = {}
    out = [jax.ShapeDtypeStruct(shape, bf16)]
    out_specs = [ANY]
    if not opening:
        ins += [before[1], before[0]]
        in_specs += [VMEM, ANY]
        aliases = {6: 0}
    scratch = [
        pltpu.VMEM((count * B, across * B), bf16),
        pltpu.VMEM((count * B, width), bf16),
        pltpu.SemaphoreType.DMA,
    ]
    if shards:
        rows = times // shards
        out.append(jax.ShapeDtypeStruct((rows, width), f32))
        out += [jax.ShapeDtypeStruct((rows + PAD, width), i16)] * (shards - 1)
        out_specs += [VMEM] * shards
        scratch.append(pltpu.VMEM((times, width), f32))
    else:
        out.append(jax.ShapeDtypeStruct((width, times), f32))
        out_specs.append(VMEM)
    return pl.pallas_call(
        functools.partial(v_body, first, count, across, opening, shards),
        out_shape=out,
        in_specs=in_specs,
        out_specs=out_specs,
        input_output_aliases=aliases,
        scratch_shapes=scratch,
        compiler_params=params(),
        cost_estimate=SMALL,
        name=f"v_pass_{first}",
    )(*ins)


def last_body(v_ref, low, high, own, *refs):
    codes, out, wide = refs[:-2], refs[-2], refs[-1]
    times = v_ref.shape[0]
    rows = out.shape[0]
    group = min(rows, B)
    wide[:PAD, :] = low[...]
    wide[PAD : PAD + times, :] = v_ref[...]
    wide[PAD + times :, :] = high[...]
    start = pl.multiple_of(lax.axis_index("svc") * rows, 16)
    window = wide[pl.ds(start, rows + 2 * PAD), :].astype(f32)
    old = window[PAD : PAD + rows]
    lap = 2.0 * old - window[PAD - 1 : PAD - 1 + rows] - window[PAD + 1 : PAD + 1 + rows]
    for g in range(rows // group):
        at = slice(g * group, (g + 1) * group)
        grad = own[at, :]
        for code in codes:
            grad = grad + decode(code, g, group)
        out[at, :] = (old[at] - step_v * (grad + ridge * old[at] + smooth * lap[at])).astype(bf16)


def last_step(v, low, high, own, codes):
    return pl.pallas_call(
        last_body,
        out_shape=jax.ShapeDtypeStruct(own.shape, bf16),
        in_specs=[VMEM] * (4 + len(codes)),
        out_specs=VMEM,
        scratch_shapes=[pltpu.VMEM((v.shape[0] + 2 * PAD, v.shape[1]), bf16)],
        compiler_params=params(),
        name="last_step",
    )(v, low, high, own, *codes)


def join_body(*refs):
    out = refs[-1]
    rows = refs[0].shape[0]
    for d, part in enumerate(refs[:-1]):
        there = jnp.bitwise_xor(lax.axis_index("svc"), d)
        out[pl.ds(pl.multiple_of(there * rows, 16), rows), :] = part[...]


def join(parts):
    rows, width = parts[0].shape
    return pl.pallas_call(
        join_body,
        out_shape=jax.ShapeDtypeStruct((rows * len(parts), width), bf16),
        in_specs=[VMEM] * len(parts),
        out_specs=VMEM,
        compiler_params=params(),
        name="join",
    )(*parts)


def swap(x, axis, mask):
    return lax.ppermute(x, axis, [(i, i ^ mask) for i in range(lax.axis_size(axis))])


def shift(x, axis, by):
    n = lax.axis_size(axis)
    return lax.ppermute(x, axis, [(i, (i + by) % n) for i in range(n)])


def chunks_of(down):
    unit = down // 8
    sizes = [unit, 2 * unit, 2 * unit, 2 * unit]
    sizes.append(down - sum(sizes))
    return [(sum(sizes[:i]), size) for i, size in enumerate(sizes)]


def on_device(u, v, block_rows, block_cols, block_counts, block_values):
    down, across = u.shape[0] // B, v.shape[0] // B
    values = block_values[0, 0]
    steps, peers = lax.axis_size("step"), lax.axis_size("svc")
    low = shift(v[-PAD:], "step", 1)
    high = shift(v[:PAD], "step", -1)
    chunks = chunks_of(down)
    keep, send, slots = first_u_pass(chunks[0][1], down, across, (block_rows, block_cols, block_counts), u, v, values)
    codes = [core_sum(keep, swap(send, "step", 1), [])]
    waiting = None
    for first, count in chunks[1:]:
        keep, send = u_pass(first, count, across, slots, u, v, values, codes[-1:])
        if waiting:
            codes.append(core_sum(*waiting, [keep]))
        waiting = (keep, swap(send, "step", 1))
    codes.append(core_sum(*waiting, codes[-1:]))
    arrived = []
    for code in codes:
        code_in = swap(code, "step", 2)
        mask = 4
        while mask < steps:
            code = chip_sum(code, code_in)
            code_in = swap(code, "step", mask)
            mask *= 2
        arrived.append((code, code_in))
    before = None
    for i, (first, count) in enumerate(chunks):
        after = [codes[-1]] if before is None else [before[1]]
        if i == len(chunks) - 1:
            after += [low, high]
        half = update(first, *arrived[i], u, after)
        halves = (half, swap(half, "step", 1))
        shards = peers if i == len(chunks) - 1 else 0
        before = v_pass(first, count, across, slots, u.shape, v, values, halves, before, shards)
    new_services, own, sent = before[0], before[1], before[2:]
    part = last_step(v, low, high, own, [swap(x, "svc", d + 1) for d, x in enumerate(sent)])
    column = [part] + [swap(part, "svc", d) for d in range(2, peers, 2)]
    return new_services, join([x for y in column for x in (y, swap(y, "svc", 1))])


def solution(mesh):
    return jax.shard_map(
        on_device,
        mesh=mesh,
        in_specs=(
            P("svc", None),
            P("step", None),
            P("svc", "step", None),
            P("svc", "step", None),
            P("svc", "step"),
            P("svc", "step", None, None, None),
        ),
        out_specs=(P("svc", None), P("step", None)),
        check_vma=False,
    )
```

```python
import functools

import jax
import jax.numpy as jnp
from jax import lax
from jax.experimental import pallas as pl
from jax.experimental.pallas import tpu as pltpu
from jax.sharding import PartitionSpec as P

step_u = 0.03
step_v = 0.02
ridge = 0.1
smooth = 20.0

f32, bf16, i32, i16 = jnp.float32, jnp.bfloat16, jnp.int32, jnp.int16
B = 128
PAD = 16
TOP = 32000.0
ROWS_BY_ROWS = (((1,), (1,)), ((), ()))
COLS_BY_COLS = (((0,), (0,)), ((), ()))

SMEM = pl.BlockSpec(memory_space=pltpu.SMEM)
VMEM = pl.BlockSpec(memory_space=pltpu.VMEM)
ANY = pl.BlockSpec(memory_space=pl.ANY)


SMALL = pl.CostEstimate(flops=1, bytes_accessed=1, transcendentals=0)


def params():
    return pltpu.CompilerParams(vmem_limit_bytes=24 * 2**20)


def encode(x):
    rows, width = x.shape
    group = min(rows, B)
    line = lax.broadcasted_iota(i32, (PAD, width), 0)
    powers = jnp.zeros((PAD, width), f32)
    parts = []
    for g in range(rows // group):
        part = x[g * group : (g + 1) * group]
        top = jnp.max(jnp.abs(part), axis=0, keepdims=True)
        power = jnp.ceil(jnp.log2(jnp.maximum(top, 1e-30)))
        parts.append(jnp.round(part * (jnp.exp2(-power) * TOP)))
        powers = jnp.where(line == g, power, powers)
    return [p.astype(i32).astype(i16) for p in parts], powers.astype(i32).astype(i16)


def store_code(ref, x):
    parts, powers = encode(x)
    group = parts[0].shape[0]
    for g, part in enumerate(parts):
        ref[g * group : (g + 1) * group, :] = part
    ref[x.shape[0] :, :] = powers


def decode(ref, g, group):
    rows = ref.shape[0] - PAD
    powers = ref[rows:, :].astype(i32).astype(f32)[g : g + 1]
    return ref[g * group : (g + 1) * group, :].astype(i32).astype(f32) * (
        jnp.exp2(powers) * (1.0 / TOP)
    )


def my_core():
    return lax.rem(lax.axis_index("step"), 2)


def two_halves(rows):
    half = rows // 2
    core = my_core()
    return [pl.ds(pl.multiple_of(at * half, 16), half) for at in (core, 1 - core)]


def residual(left, v_ref, block, err, slots, first, count, across):
    wide = min(2, across)
    for t in range(0, across, wide):
        predicted = lax.dot_general(
            left, v_ref[t * B : (t + wide) * B, :], ROWS_BY_ROWS, preferred_element_type=f32
        )
        for r in range(count):
            rows = slice(r * B, (r + 1) * B)
            for c in range(t, t + wide):
                slot = slots[(first + r) * across + c]
                gap = predicted[rows, (c - t) * B : (c - t + 1) * B] - block(slot, r, c).astype(f32)
                err[rows, c * B : (c + 1) * B] = jnp.where(slot >= 0, gap, 0.0).astype(bf16)


def split_product(err, v_ref, outs):
    for out, rows in zip((outs[:1], outs[1:]), two_halves(err.shape[0])):
        whole = jnp.dot(err[rows, :], v_ref[...], preferred_element_type=f32)
        size = out[0].shape[0]
        for i, piece in enumerate(out):
            piece[...] = whole[i * size : (i + 1) * size]


def first_u_body(
    count, down, across, row_hbm, col_hbm, live_hbm, u_hbm, v_hbm, values,
    keep, send, slots, row_ref, col_ref, live_ref, dense, err, left, v_ref, sems
):
    loads = [
        pltpu.make_async_copy(src, dst, sems.at[i])
        for i, (src, dst) in enumerate(
            (
                (row_hbm, row_ref),
                (col_hbm, col_ref),
                (live_hbm, live_ref),
                (u_hbm.at[pl.ds(0, count * B)], left),
                (v_hbm, v_ref),
            )
        )
    ]
    for load in loads:
        load.start()

    def clear(i, c):
        slots[i] = jnp.int32(-1)
        return c

    lax.fori_loop(0, down * across, clear, 0, unroll=8)
    for load in loads[:3]:
        load.wait()
    live = live_ref[0, 0]

    def enter(k, c):
        slots[row_ref[0, 0, k] * across + col_ref[0, 0, k]] = jnp.where(k < live, k, -1)
        return c

    lax.fori_loop(0, row_ref.shape[2], enter, 0, unroll=7)
    sem = sems.at[len(loads)]

    def fetch(i, started):
        slot = slots[i]

        @pl.when(slot >= 0)
        def _():
            row = pl.multiple_of((i // across) * B, B)
            pltpu.make_async_copy(
                values.at[slot], dense.at[lax.rem(i, across), pl.ds(row, B)], sem
            ).start()

        return started + (slot >= 0).astype(i32)

    started = lax.fori_loop(0, count * across, fetch, jnp.int32(0), unroll=across)
    for load in loads[3:]:
        load.wait()

    def wait(_, c):
        pltpu.make_async_copy(values.at[0], dense.at[0, pl.ds(0, B)], sem).wait()
        return c

    lax.fori_loop(0, started, wait, 0)
    block = lambda slot, r, c: dense[c, r * B : (r + 1) * B, :]
    residual(left[...], v_ref, block, err, slots, 0, count, across)
    split_product(err, v_ref, (keep, send))


def in_hbm(x):
    return pltpu.with_memory_space_constraint(x, pltpu.HBM)


def first_u_pass(count, down, across, index, u, v, values):
    rows, width = count * B, u.shape[1]
    hbm = pl.BlockSpec(memory_space=pltpu.HBM)
    part = jax.ShapeDtypeStruct((rows // 2, width), f32)
    return pl.pallas_call(
        functools.partial(first_u_body, count, down, across),
        out_shape=[part, part, jax.ShapeDtypeStruct((down * across,), i32)],
        in_specs=[hbm, hbm, ANY, hbm, hbm, hbm],
        out_specs=[VMEM, VMEM, SMEM],
        scratch_shapes=[
            *(pltpu.SMEM(x.shape, i32) for x in index),
            pltpu.VMEM((across, rows, B), bf16),
            pltpu.VMEM((rows, across * B), bf16),
            pltpu.VMEM((rows, width), bf16),
            pltpu.VMEM(v.shape, bf16),
            pltpu.SemaphoreType.DMA((6,)),
        ],
        compiler_params=params(),
        cost_estimate=SMALL,
        name="u_pass_0",
    )(*(in_hbm(x) for x in index[:2]), index[2], *(in_hbm(x) for x in (u, v, values)))


def u_body(first, count, across, waits, slots, u_ref, v_ref, values, *refs):
    outs, err = refs[waits:-1], refs[-1]
    block = lambda slot, r, c: values[jnp.maximum(slot, 0)]
    residual(u_ref[first * B : (first + count) * B, :], v_ref, block, err, slots, first, count, across)
    split_product(err, v_ref, outs)


def u_pass(first, count, across, pieces, slots, u, v, values, after):
    rows, width = count * B, u.shape[1]
    part = jax.ShapeDtypeStruct((rows // 2, width), f32)
    piece = jax.ShapeDtypeStruct((rows // 2 // pieces, width), f32)
    return pl.pallas_call(
        functools.partial(u_body, first, count, across, len(after)),
        out_shape=[part] + [piece] * pieces,
        in_specs=[SMEM, VMEM, VMEM, VMEM] + [ANY] * len(after),
        out_specs=[VMEM] * (1 + pieces),
        scratch_shapes=[pltpu.VMEM((rows, across * B), bf16)],
        compiler_params=params(),
        cost_estimate=SMALL,
        name=f"u_pass_{first}",
    )(slots, u, v, values, *after)


def sum_body(own, *refs):
    store_code(refs[-1], own[...] + jnp.concatenate([x[...] for x in refs[:-1]], axis=0))


def core_sum(own, others):
    rows, width = own.shape
    return pl.pallas_call(
        sum_body,
        out_shape=jax.ShapeDtypeStruct((rows + PAD, width), i16),
        in_specs=[VMEM] * (1 + len(others)),
        out_specs=VMEM,
        compiler_params=params(),
        cost_estimate=SMALL,
        name="core_sum",
    )(own, *others)


def again_body(mine, mine_in, out):
    rows = mine.shape[0] - PAD
    group = min(rows, B)
    whole = [decode(mine, g, group) + decode(mine_in, g, group) for g in range(rows // group)]
    store_code(out, jnp.concatenate(whole, axis=0))


def chip_sum(code, code_in):
    return pl.pallas_call(
        again_body,
        out_shape=jax.ShapeDtypeStruct(code.shape, i16),
        in_specs=[VMEM, VMEM],
        out_specs=VMEM,
        compiler_params=params(),
        name="chip_sum",
    )(code, code_in)


def update_body(first, code, code_in, u_ref, *refs):
    out = refs[-1]
    half = out.shape[0]
    group = min(half, B)
    start = first * B + my_core() * half
    for g in range(half // group):
        old = u_ref[pl.ds(pl.multiple_of(start + g * group, 16), group), :].astype(f32)
        grad = decode(code, g, group) + decode(code_in, g, group)
        out[g * group : (g + 1) * group, :] = (old - step_u * (grad + ridge * old)).astype(bf16)


def update(first, code, code_in, u, after):
    rows, width = code.shape[0] - PAD, code.shape[1]
    return pl.pallas_call(
        functools.partial(update_body, first),
        out_shape=jax.ShapeDtypeStruct((rows, width), bf16),
        in_specs=[VMEM, VMEM, VMEM] + [ANY] * len(after),
        out_specs=VMEM,
        compiler_params=params(),
        cost_estimate=SMALL,
        name=f"update_{first}",
    )(code, code_in, u, *after)


def v_body(first, count, across, opening, shards, *refs):
    slots, v_ref, values, own, other = refs[:5]
    refs = refs[5:]
    if not opening:
        before = refs[0]
        refs = refs[2:]
    new_out, refs = refs[0], refs[1:]
    if shards:
        own_out, sent, refs = refs[0], refs[1:shards], refs[shards:]
    else:
        total, refs = refs[0], refs[1:]
    err, left, sem = refs[:3]
    for src, rows in zip((own, other), two_halves(count * B)):
        left[rows, :] = src[...]
    save = pltpu.make_async_copy(left, new_out.at[pl.ds(first * B, count * B)], sem)
    save.start()
    block = lambda slot, r, c: values[jnp.maximum(slot, 0)]
    residual(left[...], v_ref, block, err, slots, first, count, across)
    part = lax.dot_general(left[...], err[...], COLS_BY_COLS, preferred_element_type=f32)
    if not opening:
        part = part + before[...]
    if not shards:
        total[...] = part
    else:
        turned = refs[3]
        turned[...] = part.T
        rows = turned.shape[0] // shards
        here = lax.axis_index("svc")
        own_out[...] = turned[pl.ds(pl.multiple_of(here * rows, 8), rows), :]
        for d in range(1, shards):
            there = jnp.bitwise_xor(here, d)
            store_code(sent[d - 1], turned[pl.ds(pl.multiple_of(there * rows, 8), rows), :])
    save.wait()


def v_pass(first, count, across, slots, shape, v, values, halves, before, shards):
    width = v.shape[1]
    times = v.shape[0]
    opening = before is None
    ins = [slots, v, values, *halves]
    in_specs = [SMEM] + [VMEM] * 4
    aliases = {}
    out = [jax.ShapeDtypeStruct(shape, bf16)]
    out_specs = [ANY]
    if not opening:
        ins += [before[1], before[0]]
        in_specs += [VMEM, ANY]
        aliases = {6: 0}
    scratch = [
        pltpu.VMEM((count * B, across * B), bf16),
        pltpu.VMEM((count * B, width), bf16),
        pltpu.SemaphoreType.DMA,
    ]
    if shards:
        rows = times // shards
        out.append(jax.ShapeDtypeStruct((rows, width), f32))
        out += [jax.ShapeDtypeStruct((rows + PAD, width), i16)] * (shards - 1)
        out_specs += [VMEM] * shards
        scratch.append(pltpu.VMEM((times, width), f32))
    else:
        out.append(jax.ShapeDtypeStruct((width, times), f32))
        out_specs.append(VMEM)
    return pl.pallas_call(
        functools.partial(v_body, first, count, across, opening, shards),
        out_shape=out,
        in_specs=in_specs,
        out_specs=out_specs,
        input_output_aliases=aliases,
        scratch_shapes=scratch,
        compiler_params=params(),
        cost_estimate=SMALL,
        name=f"v_pass_{first}",
    )(*ins)


def last_body(v_ref, low, high, own, *refs):
    codes, out, wide = refs[:-2], refs[-2], refs[-1]
    times = v_ref.shape[0]
    rows = out.shape[0]
    group = min(rows, B)
    wide[:PAD, :] = low[...]
    wide[PAD : PAD + times, :] = v_ref[...]
    wide[PAD + times :, :] = high[...]
    start = pl.multiple_of(lax.axis_index("svc") * rows, 16)
    window = wide[pl.ds(start, rows + 2 * PAD), :].astype(f32)
    old = window[PAD : PAD + rows]
    lap = 2.0 * old - window[PAD - 1 : PAD - 1 + rows] - window[PAD + 1 : PAD + 1 + rows]
    for g in range(rows // group):
        at = slice(g * group, (g + 1) * group)
        grad = own[at, :]
        for code in codes:
            grad = grad + decode(code, g, group)
        out[at, :] = (old[at] - step_v * (grad + ridge * old[at] + smooth * lap[at])).astype(bf16)


def last_step(v, low, high, own, codes):
    return pl.pallas_call(
        last_body,
        out_shape=jax.ShapeDtypeStruct(own.shape, bf16),
        in_specs=[VMEM] * (4 + len(codes)),
        out_specs=VMEM,
        scratch_shapes=[pltpu.VMEM((v.shape[0] + 2 * PAD, v.shape[1]), bf16)],
        compiler_params=params(),
        name="last_step",
    )(v, low, high, own, *codes)


def join_body(*refs):
    out = refs[-1]
    rows = refs[0].shape[0]
    for d, part in enumerate(refs[:-1]):
        there = jnp.bitwise_xor(lax.axis_index("svc"), d)
        out[pl.ds(pl.multiple_of(there * rows, 16), rows), :] = part[...]


def join(parts):
    rows, width = parts[0].shape
    return pl.pallas_call(
        join_body,
        out_shape=jax.ShapeDtypeStruct((rows * len(parts), width), bf16),
        in_specs=[VMEM] * len(parts),
        out_specs=VMEM,
        compiler_params=params(),
        name="join",
    )(*parts)


def swap(x, axis, mask):
    return lax.ppermute(x, axis, [(i, i ^ mask) for i in range(lax.axis_size(axis))])


def shift(x, axis, by):
    n = lax.axis_size(axis)
    return lax.ppermute(x, axis, [(i, (i + by) % n) for i in range(n)])


def chunks_of(down):
    unit = down // 8
    sizes = [unit, 2 * unit, 2 * unit, 2 * unit]
    sizes.append(down - sum(sizes))
    return [(sum(sizes[:i]), size) for i, size in enumerate(sizes)]


def on_device(u, v, block_rows, block_cols, block_counts, block_values):
    down, across = u.shape[0] // B, v.shape[0] // B
    values = block_values[0, 0]
    steps, peers = lax.axis_size("step"), lax.axis_size("svc")
    low = shift(v[-PAD:], "step", 1)
    high = shift(v[:PAD], "step", -1)
    chunks = chunks_of(down)
    keep, send, slots = first_u_pass(chunks[0][1], down, across, (block_rows, block_cols, block_counts), u, v, values)
    codes = [core_sum(keep, [swap(send, "step", 1)])]
    arrived, halves = [], []
    before = None
    last = len(chunks) - 1

    def cross(k):
        code, mask = codes[k], 4
        code_in = swap(code, "step", 2)
        while mask < steps:
            code = chip_sum(code, code_in)
            code_in = swap(code, "step", mask)
            mask *= 2
        arrived.append((code, code_in))

    def renew(k, after):
        half = update(chunks[k][0], *arrived[k], u, after)
        halves.append((half, swap(half, "step", 1)))

    cross(0)
    token = codes[0]
    for k in range(1, last + 2):
        if k <= last:
            first, count = chunks[k]
            pieces = pl.cdiv(2 * count, chunks[k - 1][1])
            while count * B // 2 % (8 * pieces):
                pieces += 1
            keep, *send = u_pass(first, count, across, pieces, slots, u, v, values, [token])
            codes.append(core_sum(keep, [swap(x, "step", 1) for x in send]))
            cross(k)
        if k >= 2:
            first, count = chunks[k - 2]
            before = v_pass(first, count, across, slots, u.shape, v, values, halves[k - 2], before, 0)
        renew(k - 1, [codes[-1]] + ([before[1]] if before else []) + ([low, high] if k > last else []))
        token = halves[k - 1][0]
    first, count = chunks[last]
    before = v_pass(first, count, across, slots, u.shape, v, values, halves[last], before, peers)
    new_services, own, sent = before[0], before[1], before[2:]
    far_first = sorted(range(1, peers), reverse=True)
    part = last_step(v, low, high, own, [swap(sent[d - 1], "svc", d) for d in far_first])
    column = {0: part}
    for d in far_first:
        if d % 2 == 0:
            column[d] = swap(part, "svc", d)
    for d in (0, *(x for x in far_first if x % 2 == 0)):
        column[d + 1] = swap(column[d], "svc", 1)
    return new_services, join([column[d] for d in range(peers)])


def solution(mesh):
    return jax.shard_map(
        on_device,
        mesh=mesh,
        in_specs=(
            P("svc", None),
            P("step", None),
            P("svc", "step", None),
            P("svc", "step", None),
            P("svc", "step"),
            P("svc", "step", None, None, None),
        ),
        out_specs=(P("svc", None), P("step", None)),
        check_vma=False,
    )
```

```python
import functools

import jax
import jax.numpy as jnp
from jax import lax
from jax.experimental import pallas as pl
from jax.experimental.pallas import tpu as pltpu
from jax.sharding import PartitionSpec as P

step_u = 0.03
step_v = 0.02
ridge = 0.1
smooth = 20.0

f32, bf16, i32, i16 = jnp.float32, jnp.bfloat16, jnp.int32, jnp.int16
B = 128
PAD = 16
TOP = 32000.0
ROWS_BY_ROWS = (((1,), (1,)), ((), ()))
COLS_BY_COLS = (((0,), (0,)), ((), ()))

SMEM = pl.BlockSpec(memory_space=pltpu.SMEM)
VMEM = pl.BlockSpec(memory_space=pltpu.VMEM)
ANY = pl.BlockSpec(memory_space=pl.ANY)


SMALL = pl.CostEstimate(flops=1, bytes_accessed=1, transcendentals=0)


def params():
    return pltpu.CompilerParams(vmem_limit_bytes=24 * 2**20)


def encode(x):
    rows, width = x.shape
    group = min(rows, B)
    line = lax.broadcasted_iota(i32, (PAD, width), 0)
    powers = jnp.zeros((PAD, width), f32)
    parts = []
    for g in range(rows // group):
        part = x[g * group : (g + 1) * group]
        top = jnp.max(jnp.abs(part), axis=0, keepdims=True)
        power = jnp.ceil(jnp.log2(jnp.maximum(top, 1e-30)))
        parts.append(jnp.round(part * (jnp.exp2(-power) * TOP)))
        powers = jnp.where(line == g, power, powers)
    return [p.astype(i32).astype(i16) for p in parts], powers.astype(i32).astype(i16)


def store_code(ref, x):
    parts, powers = encode(x)
    group = parts[0].shape[0]
    for g, part in enumerate(parts):
        ref[g * group : (g + 1) * group, :] = part
    ref[x.shape[0] :, :] = powers


def decode(ref, g, group):
    rows = ref.shape[0] - PAD
    powers = ref[rows:, :].astype(i32).astype(f32)[g : g + 1]
    return ref[g * group : (g + 1) * group, :].astype(i32).astype(f32) * (
        jnp.exp2(powers) * (1.0 / TOP)
    )


def my_core():
    return lax.rem(lax.axis_index("step"), 2)


def two_halves(rows):
    half = rows // 2
    core = my_core()
    return [pl.ds(pl.multiple_of(at * half, 16), half) for at in (core, 1 - core)]


def residual(left, v_ref, block, err, slots, first, count, across, base=0, ready=None):
    columns = err.shape[1] // B
    wide = min(2, columns)
    for t in range(0, columns, wide):
        start = t * B if isinstance(base, int) else pl.multiple_of((base + t) * B, B)
        predicted = lax.dot_general(
            left, v_ref[pl.ds(start, wide * B), :], ROWS_BY_ROWS, preferred_element_type=f32
        )
        if ready:
            ready(t, wide)
        for r in range(count):
            rows = slice(r * B, (r + 1) * B)
            for c in range(t, t + wide):
                slot = slots[(first + r) * across + base + c]
                gap = predicted[rows, (c - t) * B : (c - t + 1) * B] - block(slot, r, c).astype(f32)
                err[rows, c * B : (c + 1) * B] = jnp.where(slot >= 0, gap, 0.0).astype(bf16)


def split_product(err, v_ref, outs):
    for out, rows in zip((outs[:1], outs[1:]), two_halves(err.shape[0])):
        whole = jnp.dot(err[rows, :], v_ref[...], preferred_element_type=f32)
        size = out[0].shape[0]
        for i, piece in enumerate(out):
            piece[...] = whole[i * size : (i + 1) * size]


def first_u_body(
    count, down, across, row_hbm, col_hbm, live_ref, u_hbm, v_hbm, values,
    keep, send, slots, row_ref, col_ref, dense, err, left, v_ref, sems
):
    loads = [
        pltpu.make_async_copy(src, dst, sems.at[i])
        for i, (src, dst) in enumerate(
            (
                (row_hbm, row_ref),
                (col_hbm, col_ref),
                (u_hbm.at[pl.ds(0, count * B)], left),
                (v_hbm, v_ref),
            )
        )
    ]
    for load in loads:
        load.start()

    def clear(i, c):
        slots[i] = jnp.int32(-1)
        return c

    lax.fori_loop(0, down * across, clear, 0, unroll=8)
    for load in loads[:2]:
        load.wait()
    live = live_ref[0, 0]

    total = row_ref.shape[2]
    batch = next(n for n in (14, 11, 8, 7, 4, 2, 1) if total % n == 0)

    def enter(i, c):
        at = [i * batch + j for j in range(batch)]
        where = [row_ref[0, 0, k] * across + col_ref[0, 0, k] for k in at]
        for k, place in zip(at, where):
            slots[place] = jnp.where(k < live, k, -1)
        return c

    lax.fori_loop(0, total // batch, enter, 0)
    sem = sems.at[len(loads)]

    def fetch(c):
        def go(r, started):
            slot = slots[r * across + c]

            @pl.when(slot >= 0)
            def _():
                row = pl.multiple_of(r * B, B)
                pltpu.make_async_copy(values.at[slot], dense.at[c, pl.ds(row, B)], sem).start()

            return started + (slot >= 0).astype(i32)

        return lax.fori_loop(0, count, go, jnp.int32(0), unroll=True)

    started = sum(fetch(c) for c in range(across))
    for load in loads[2:]:
        load.wait()

    def wait(_, c):
        pltpu.make_async_copy(values.at[0], dense.at[0, pl.ds(0, B)], sem).wait()
        return c

    def ready(t, wide):
        if t == 0:
            lax.fori_loop(0, started, wait, 0)

    block = lambda slot, r, c: dense[c, r * B : (r + 1) * B, :]
    residual(left[...], v_ref, block, err, slots, 0, count, across, 0, ready)
    split_product(err, v_ref, (keep, send))


def in_hbm(x):
    return pltpu.with_memory_space_constraint(x, pltpu.HBM)


def first_u_pass(count, down, across, index, u, v, values):
    rows, width = count * B, u.shape[1]
    hbm = pl.BlockSpec(memory_space=pltpu.HBM)
    part = jax.ShapeDtypeStruct((rows // 2, width), f32)
    return pl.pallas_call(
        functools.partial(first_u_body, count, down, across),
        out_shape=[part, part, jax.ShapeDtypeStruct((down * across,), i32)],
        in_specs=[hbm, hbm, SMEM, hbm, hbm, hbm],
        out_specs=[VMEM, VMEM, SMEM],
        scratch_shapes=[
            *(pltpu.SMEM(x.shape, i32) for x in index[:2]),
            pltpu.VMEM((across, rows, B), bf16),
            pltpu.VMEM((rows, across * B), bf16),
            pltpu.VMEM((rows, width), bf16),
            pltpu.VMEM(v.shape, bf16),
            pltpu.SemaphoreType.DMA((5,)),
        ],
        compiler_params=params(),
        cost_estimate=SMALL,
        name="u_pass_0",
    )(*(in_hbm(x) for x in index[:2]), index[2], *(in_hbm(x) for x in (u, v, values)))


def u_body(first, count, across, waits, slots, u_ref, v_ref, values, *refs):
    outs, err = refs[waits:-1], refs[-1]
    block = lambda slot, r, c: values[jnp.maximum(slot, 0)]
    residual(u_ref[first * B : (first + count) * B, :], v_ref, block, err, slots, first, count, across)
    split_product(err, v_ref, outs)


def u_pass(first, count, across, pieces, slots, u, v, values, after):
    rows, width = count * B, u.shape[1]
    part = jax.ShapeDtypeStruct((rows // 2, width), f32)
    piece = jax.ShapeDtypeStruct((rows // 2 // pieces, width), f32)
    return pl.pallas_call(
        functools.partial(u_body, first, count, across, len(after)),
        out_shape=[part] + [piece] * pieces,
        in_specs=[SMEM, VMEM, VMEM, VMEM] + [ANY] * len(after),
        out_specs=[VMEM] * (1 + pieces),
        scratch_shapes=[pltpu.VMEM((rows, across * B), bf16)],
        compiler_params=params(),
        cost_estimate=SMALL,
        name=f"u_pass_{first}",
    )(slots, u, v, values, *after)


def sum_body(own, *refs):
    store_code(refs[-1], own[...] + jnp.concatenate([x[...] for x in refs[:-1]], axis=0))


def core_sum(own, others):
    rows, width = own.shape
    return pl.pallas_call(
        sum_body,
        out_shape=jax.ShapeDtypeStruct((rows + PAD, width), i16),
        in_specs=[VMEM] * (1 + len(others)),
        out_specs=VMEM,
        compiler_params=params(),
        cost_estimate=SMALL,
        name="core_sum",
    )(own, *others)


def again_body(mine, mine_in, out):
    rows = mine.shape[0] - PAD
    group = min(rows, B)
    whole = [decode(mine, g, group) + decode(mine_in, g, group) for g in range(rows // group)]
    store_code(out, jnp.concatenate(whole, axis=0))


def chip_sum(code, code_in):
    return pl.pallas_call(
        again_body,
        out_shape=jax.ShapeDtypeStruct(code.shape, i16),
        in_specs=[VMEM, VMEM],
        out_specs=VMEM,
        compiler_params=params(),
        name="chip_sum",
    )(code, code_in)


def update_body(first, code, code_in, u_ref, *refs):
    out = refs[-1]
    half = out.shape[0]
    group = min(half, B)
    start = first * B + my_core() * half
    for g in range(half // group):
        old = u_ref[pl.ds(pl.multiple_of(start + g * group, 16), group), :].astype(f32)
        grad = decode(code, g, group) + decode(code_in, g, group)
        out[g * group : (g + 1) * group, :] = (old - step_u * (grad + ridge * old)).astype(bf16)


def update(first, code, code_in, u, after):
    rows, width = code.shape[0] - PAD, code.shape[1]
    return pl.pallas_call(
        functools.partial(update_body, first),
        out_shape=jax.ShapeDtypeStruct((rows, width), bf16),
        in_specs=[VMEM, VMEM, VMEM] + [ANY] * len(after),
        out_specs=VMEM,
        compiler_params=params(),
        cost_estimate=SMALL,
        name=f"update_{first}",
    )(code, code_in, u, *after)


def gather_left(left, own, others):
    mine, theirs = two_halves(left.shape[0])
    left[mine, :] = own[...]
    size = others[0].shape[0]
    for i, piece in enumerate(others):
        left[pl.ds(pl.multiple_of(theirs.start + i * size, 16), size), :] = piece[...]


def v_body(first, count, across, opening, pieces, *refs):
    slots, v_ref, values, own = refs[:4]
    others, refs = refs[4 : 4 + pieces], refs[4 + pieces :]
    if not opening:
        before = refs[0]
        refs = refs[2:]
    new_out, total, err, left, sem = refs
    gather_left(left, own, others)
    save = pltpu.make_async_copy(left, new_out.at[pl.ds(first * B, count * B)], sem)
    save.start()
    block = lambda slot, r, c: values[jnp.maximum(slot, 0)]
    residual(left[...], v_ref, block, err, slots, first, count, across)
    part = lax.dot_general(left[...], err[...], COLS_BY_COLS, preferred_element_type=f32)
    if not opening:
        part = part + before[...]
    total[...] = part
    save.wait()


def v_pass(first, count, across, slots, shape, v, values, halves, before):
    width = v.shape[1]
    times = v.shape[0]
    opening = before is None
    ins = [slots, v, values, *halves]
    in_specs = [SMEM] + [VMEM] * (2 + len(halves))
    aliases = {}
    if not opening:
        aliases = {len(ins) + 1: 0}
        ins += [before[1], before[0]]
        in_specs += [VMEM, ANY]
    return pl.pallas_call(
        functools.partial(v_body, first, count, across, opening, len(halves) - 1),
        out_shape=[jax.ShapeDtypeStruct(shape, bf16), jax.ShapeDtypeStruct((width, times), f32)],
        in_specs=in_specs,
        out_specs=[ANY, VMEM],
        input_output_aliases=aliases,
        scratch_shapes=[
            pltpu.VMEM((count * B, across * B), bf16),
            pltpu.VMEM((count * B, width), bf16),
            pltpu.SemaphoreType.DMA,
        ],
        compiler_params=params(),
        cost_estimate=SMALL,
        name=f"v_pass_{first}",
    )(*ins)


def v_end_body(first, count, across, peers, far, pieces, kinds, *refs):
    slots, v_ref, values, own = refs[:4]
    others, before, refs = refs[4 : 4 + pieces], refs[4 + pieces], refs[5 + pieces :]
    if far:
        new_out, outs = refs[1], refs[2 : 2 + len(kinds)]
    else:
        outs = refs[1 : 1 + len(kinds)]
    err, left, turned, sem = refs[-4:]
    here = lax.axis_index("svc")
    side = lax.div(here, peers // 2)
    base = (1 - side if far else side) * (across // 2)
    gather_left(left, own, others)
    if far:
        save = pltpu.make_async_copy(left, new_out.at[pl.ds(first * B, count * B)], sem)
        save.start()
    block = lambda slot, r, c: values[jnp.maximum(slot, 0)]
    residual(left[...], v_ref, block, err, slots, first, count, across, base)
    part = lax.dot_general(left[...], err[...], COLS_BY_COLS, preferred_element_type=f32)
    part = part + before[:, pl.ds(pl.multiple_of(base * B, B), across // 2 * B)]
    turned[...] = part.T
    rows = turned.shape[0] // (peers // 2)
    for (d, coded), out in zip(kinds, outs):
        there = lax.rem(jnp.bitwise_xor(here, d), peers // 2)
        part = turned[pl.ds(pl.multiple_of(there * rows, 8), rows), :]
        if coded:
            store_code(out, part)
        else:
            out[...] = part
    if far:
        save.wait()


def v_end(first, count, across, peers, far, kinds, slots, v, values, halves, before, after):
    times, width = v.shape
    rows = times // peers
    ins = [slots, v, values, *halves, before[1], after if after is not None else before[0]]
    in_specs = [SMEM] + [VMEM] * (3 + len(halves)) + [ANY]
    out = [jax.ShapeDtypeStruct((rows + PAD, width), i16) if coded else jax.ShapeDtypeStruct((rows, width), f32) for _, coded in kinds]
    out_specs = [VMEM] * len(kinds)
    if far:
        out = [jax.ShapeDtypeStruct(before[0].shape, bf16)] + out
        out_specs = [ANY] + out_specs
    return pl.pallas_call(
        functools.partial(v_end_body, first, count, across, peers, far, len(halves) - 1, kinds),
        out_shape=out,
        in_specs=in_specs,
        out_specs=out_specs,
        input_output_aliases={len(ins) - 1: 0} if far else {},
        scratch_shapes=[
            pltpu.VMEM((count * B, times // 2), bf16),
            pltpu.VMEM((count * B, width), bf16),
            pltpu.VMEM((times // 2, width), f32),
            pltpu.SemaphoreType.DMA,
        ],
        compiler_params=params(),
        cost_estimate=SMALL,
        name="v_end_far" if far else "v_end_near",
    )(*ins)


def combine_body(joined, *refs):
    outs = refs[(len(refs) + joined) // 2 :]
    owns, codes = refs[: len(outs)], refs[len(outs) : len(outs) + joined]
    for i, (own, out) in enumerate(zip(owns, outs)):
        if i < joined:
            group = min(own.shape[0], B)
            sums = [
                own[g * group : (g + 1) * group, :] + decode(codes[i], g, group)
                for g in range(own.shape[0] // group)
            ]
            store_code(out, jnp.concatenate(sums, axis=0))
        else:
            store_code(out, own[...])


def combine(owns, codes):
    rows, width = owns[0].shape
    return pl.pallas_call(
        functools.partial(combine_body, len(codes)),
        out_shape=[jax.ShapeDtypeStruct((rows + PAD, width), i16)] * len(owns),
        in_specs=[VMEM] * (len(owns) + len(codes)),
        out_specs=[VMEM] * len(owns),
        compiler_params=params(),
        cost_estimate=SMALL,
        name="combine",
    )(*owns, *codes)


def last_body(v_ref, low, high, own, *refs):
    codes, out, wide = refs[:-2], refs[-2], refs[-1]
    times = v_ref.shape[0]
    rows = out.shape[0]
    group = min(rows, B)
    wide[:PAD, :] = low[...]
    wide[PAD : PAD + times, :] = v_ref[...]
    wide[PAD + times :, :] = high[...]
    start = pl.multiple_of(lax.axis_index("svc") * rows, 16)
    window = wide[pl.ds(start, rows + 2 * PAD), :].astype(f32)
    old = window[PAD : PAD + rows]
    lap = 2.0 * old - window[PAD - 1 : PAD - 1 + rows] - window[PAD + 1 : PAD + 1 + rows]
    for g in range(rows // group):
        at = slice(g * group, (g + 1) * group)
        grad = own[at, :]
        for code in codes:
            grad = grad + decode(code, g, group)
        out[at, :] = (old[at] - step_v * (grad + ridge * old[at] + smooth * lap[at])).astype(bf16)


def last_step(v, low, high, own, codes):
    return pl.pallas_call(
        last_body,
        out_shape=jax.ShapeDtypeStruct(own.shape, bf16),
        in_specs=[VMEM] * (4 + len(codes)),
        out_specs=VMEM,
        scratch_shapes=[pltpu.VMEM((v.shape[0] + 2 * PAD, v.shape[1]), bf16)],
        compiler_params=params(),
        name="last_step",
    )(v, low, high, own, *codes)


def join_body(order, *refs):
    out = refs[-1]
    rows = refs[0].shape[0]
    for d, part in zip(order, refs[:-1]):
        there = jnp.bitwise_xor(lax.axis_index("svc"), d)
        out[pl.ds(pl.multiple_of(there * rows, 16), rows), :] = part[...]


def join(parts):
    order, parts = zip(*parts.items())
    rows, width = parts[0].shape
    return pl.pallas_call(
        functools.partial(join_body, order),
        out_shape=jax.ShapeDtypeStruct((rows * len(parts), width), bf16),
        in_specs=[VMEM] * len(parts),
        out_specs=VMEM,
        compiler_params=params(),
        cost_estimate=SMALL,
        name="join",
    )(*parts)


def swap(x, axis, mask):
    return lax.ppermute(x, axis, [(i, i ^ mask) for i in range(lax.axis_size(axis))])


def shift(x, axis, by):
    n = lax.axis_size(axis)
    return lax.ppermute(x, axis, [(i, (i + by) % n) for i in range(n)])


SHARES = (3, 6, 6, 6, 3)


def chunks_of(down):
    unit = down // sum(SHARES)
    sizes = [unit * share for share in SHARES[:-1]]
    sizes.append(down - sum(sizes))
    return [(sum(sizes[:i]), size) for i, size in enumerate(sizes)]


def on_device(u, v, block_rows, block_cols, block_counts, block_values):
    down, across = u.shape[0] // B, v.shape[0] // B
    values = block_values[0, 0]
    steps, peers = lax.axis_size("step"), lax.axis_size("svc")
    low = shift(v[-PAD:], "step", 1)
    high = shift(v[:PAD], "step", -1)
    chunks = chunks_of(down)
    keep, send, slots = first_u_pass(chunks[0][1], down, across, (block_rows, block_cols, block_counts), u, v, values)
    codes = [core_sum(keep, [swap(send, "step", 1)])]
    arrived, halves = [], []
    before = None
    last = len(chunks) - 1

    def cross(k):
        code, mask = codes[k], 4
        code_in = swap(code, "step", 2)
        while mask < steps:
            code = chip_sum(code, code_in)
            code_in = swap(code, "step", mask)
            mask *= 2
        arrived.append((code, code_in))

    def renew(k, after):
        half = update(chunks[k][0], *arrived[k], u, after)
        pieces = 1 if k == last else pl.cdiv(chunks[k][1], chunks[k + 1][1])
        while half.shape[0] % (PAD * pieces):
            pieces += 1
        size = half.shape[0] // pieces
        halves.append((half, *(swap(half[i * size : (i + 1) * size], "step", 1) for i in range(pieces))))

    cross(0)
    token = codes[0]
    for k in range(1, last + 2):
        if k <= last:
            first, count = chunks[k]
            pieces = pl.cdiv(2 * count, chunks[k - 1][1])
            while count * B // 2 % (8 * pieces):
                pieces += 1
            keep, *send = u_pass(first, count, across, pieces, slots, u, v, values, [token])
            codes.append(core_sum(keep, [swap(x, "step", 1) for x in send]))
            cross(k)
        if k >= 2:
            first, count = chunks[k - 2]
            before = v_pass(first, count, across, slots, u.shape, v, values, halves[k - 2], before)
        renew(k - 1, [codes[-1]] + ([before[1]] if before else []) + ([low, high] if k > last else []))
        token = halves[k - 1][0]
    first, count = chunks[last]
    by_x = [d for d in range(peers * 3 // 4, peers) if d % 2]
    far = [(d, d + 1 not in by_x) for d in range(peers // 2, peers)]
    near = [(d, False) for d in range(peers // 2)]
    new_services, *sent = v_end(first, count, across, peers, True, far, slots, v, values, halves[last], before, None)
    sent = dict(zip((d for d, _ in far), sent))
    arrived_x = {d: swap(sent.pop(d), "svc", 1) for d in by_x}
    rest = v_end(first, count, across, peers, False, near, slots, v, values, halves[last], before, sent[peers // 2])
    own = rest[0]
    late = [d - 1 for d in by_x] + list(range(1, peers // 2))
    coded = combine([sent[d - 1] for d in by_x] + list(rest[1:]), [arrived_x[d] for d in by_x])
    sent = {d: x for d, x in sent.items() if d not in late} | dict(zip(late, coded))
    part = last_step(v, low, high, own, [swap(x, "svc", d) for d, x in sent.items()])
    column = {d: swap(part, "svc", d) for d in range(peers - 2, 0, -2)}
    column[0] = part
    for d in [x for x in column if x] + [0]:
        column[d + 1] = swap(column[d], "svc", 1)
    return new_services, join(column)


def solution(mesh):
    return jax.shard_map(
        on_device,
        mesh=mesh,
        in_specs=(
            P("svc", None),
            P("step", None),
            P("svc", "step", None),
            P("svc", "step", None),
            P("svc", "step"),
            P("svc", "step", None, None, None),
        ),
        out_specs=(P("svc", None), P("step", None)),
        check_vma=False,
    )
```

```python
import functools

import jax
import jax.numpy as jnp
from jax import lax
from jax.experimental import pallas as pl
from jax.experimental.pallas import tpu as pltpu
from jax.sharding import PartitionSpec as P

step_u = 0.03
step_v = 0.02
ridge = 0.1
smooth = 20.0

f32, bf16, i32, i16 = jnp.float32, jnp.bfloat16, jnp.int32, jnp.int16
B = 128
PAD = 16
TOP = 32000.0
ROWS_BY_ROWS = (((1,), (1,)), ((), ()))
COLS_BY_COLS = (((0,), (0,)), ((), ()))

SMEM = pl.BlockSpec(memory_space=pltpu.SMEM)
VMEM = pl.BlockSpec(memory_space=pltpu.VMEM)
ANY = pl.BlockSpec(memory_space=pl.ANY)


SMALL = pl.CostEstimate(flops=1, bytes_accessed=1, transcendentals=0)


def params():
    return pltpu.CompilerParams(vmem_limit_bytes=24 * 2**20)


def encode(x):
    rows, width = x.shape
    group = min(rows, B)
    line = lax.broadcasted_iota(i32, (PAD, width), 0)
    powers = jnp.zeros((PAD, width), f32)
    parts = []
    for g in range(rows // group):
        part = x[g * group : (g + 1) * group]
        top = jnp.max(jnp.abs(part), axis=0, keepdims=True)
        power = jnp.ceil(jnp.log2(jnp.maximum(top, 1e-30)))
        parts.append(jnp.round(part * (jnp.exp2(-power) * TOP)))
        powers = jnp.where(line == g, power, powers)
    return [p.astype(i32).astype(i16) for p in parts], powers.astype(i32).astype(i16)


def store_code(ref, x):
    parts, powers = encode(x)
    group = parts[0].shape[0]
    for g, part in enumerate(parts):
        ref[g * group : (g + 1) * group, :] = part
    ref[x.shape[0] :, :] = powers


def decode(ref, g, group):
    rows = ref.shape[0] - PAD
    powers = ref[rows:, :].astype(i32).astype(f32)[g : g + 1]
    return ref[g * group : (g + 1) * group, :].astype(i32).astype(f32) * (
        jnp.exp2(powers) * (1.0 / TOP)
    )


def my_core():
    return lax.rem(lax.axis_index("step"), 2)


def two_halves(rows):
    half = rows // 2
    core = my_core()
    return [pl.ds(pl.multiple_of(at * half, 16), half) for at in (core, 1 - core)]


def residual(left, v_ref, block, err, slots, first, count, across, base=0, ready=None):
    columns = err.shape[1] // B
    wide = min(2, columns)
    for t in range(0, columns, wide):
        start = t * B if isinstance(base, int) else pl.multiple_of((base + t) * B, B)
        predicted = lax.dot_general(
            left, v_ref[pl.ds(start, wide * B), :], ROWS_BY_ROWS, preferred_element_type=f32
        )
        if ready:
            ready(t, wide)
        for r in range(count):
            rows = slice(r * B, (r + 1) * B)
            for c in range(t, t + wide):
                slot = slots[(first + r) * across + base + c]
                gap = predicted[rows, (c - t) * B : (c - t + 1) * B] - block(slot, r, c).astype(f32)
                err[rows, c * B : (c + 1) * B] = jnp.where(slot >= 0, gap, 0.0).astype(bf16)


def split_product(err, v_ref, keep, sends):
    mine, theirs = two_halves(err.shape[0])
    whole = jnp.dot(err[theirs, :], v_ref[...], preferred_element_type=f32)
    size = whole.shape[0] // len(sends)
    for i, send in enumerate(sends):
        store_code(send, whole[i * size : (i + 1) * size])
    keep[...] = jnp.dot(err[mine, :], v_ref[...], preferred_element_type=f32)


def first_u_body(
    count, down, across, row_hbm, col_hbm, live_ref, u_hbm, v_hbm, values,
    keep, send, slots, row_ref, col_ref, dense, err, left, v_ref, sems
):
    loads = [
        pltpu.make_async_copy(src, dst, sems.at[i])
        for i, (src, dst) in enumerate(
            (
                (row_hbm, row_ref),
                (col_hbm, col_ref),
                (u_hbm.at[pl.ds(0, count * B)], left),
                (v_hbm, v_ref),
            )
        )
    ]
    for load in loads:
        load.start()

    def clear(i, c):
        slots[i] = jnp.int32(-1)
        return c

    lax.fori_loop(0, down * across, clear, 0, unroll=8)
    for load in loads[:2]:
        load.wait()
    live = live_ref[0, 0]

    total = row_ref.shape[2]
    batch = next(n for n in (14, 11, 8, 7, 4, 2, 1) if total % n == 0)

    def enter(i, c):
        at = [i * batch + j for j in range(batch)]
        where = [row_ref[0, 0, k] * across + col_ref[0, 0, k] for k in at]
        for k, place in zip(at, where):
            slots[place] = jnp.where(k < live, k, -1)
        return c

    lax.fori_loop(0, total // batch, enter, 0)
    sem = sems.at[len(loads)]

    def fetch(c):
        def go(r, started):
            slot = slots[r * across + c]

            @pl.when(slot >= 0)
            def _():
                row = pl.multiple_of(r * B, B)
                pltpu.make_async_copy(values.at[slot], dense.at[c, pl.ds(row, B)], sem).start()

            return started + (slot >= 0).astype(i32)

        return lax.fori_loop(0, count, go, jnp.int32(0), unroll=True)

    started = sum(fetch(c) for c in range(across))
    for load in loads[2:]:
        load.wait()

    def wait(_, c):
        pltpu.make_async_copy(values.at[0], dense.at[0, pl.ds(0, B)], sem).wait()
        return c

    def ready(t, wide):
        if t == 0:
            lax.fori_loop(0, started, wait, 0)

    block = lambda slot, r, c: dense[c, r * B : (r + 1) * B, :]
    residual(left[...], v_ref, block, err, slots, 0, count, across, 0, ready)
    split_product(err, v_ref, keep, [send])


def in_hbm(x):
    return pltpu.with_memory_space_constraint(x, pltpu.HBM)


def first_u_pass(count, down, across, index, u, v, values):
    rows, width = count * B, u.shape[1]
    hbm = pl.BlockSpec(memory_space=pltpu.HBM)
    part = jax.ShapeDtypeStruct((rows // 2, width), f32)
    return pl.pallas_call(
        functools.partial(first_u_body, count, down, across),
        out_shape=[part, jax.ShapeDtypeStruct((rows // 2 + PAD, width), i16), jax.ShapeDtypeStruct((down * across,), i32)],
        in_specs=[hbm, hbm, SMEM, hbm, hbm, hbm],
        out_specs=[VMEM, VMEM, SMEM],
        scratch_shapes=[
            *(pltpu.SMEM(x.shape, i32) for x in index[:2]),
            pltpu.VMEM((across, rows, B), bf16),
            pltpu.VMEM((rows, across * B), bf16),
            pltpu.VMEM((rows, width), bf16),
            pltpu.VMEM(v.shape, bf16),
            pltpu.SemaphoreType.DMA((5,)),
        ],
        compiler_params=params(),
        cost_estimate=SMALL,
        name="u_pass_0",
    )(*(in_hbm(x) for x in index[:2]), index[2], *(in_hbm(x) for x in (u, v, values)))


def u_body(first, count, across, waits, slots, u_ref, v_ref, values, *refs):
    outs, err = refs[waits:-1], refs[-1]
    block = lambda slot, r, c: values[jnp.maximum(slot, 0)]
    residual(u_ref[first * B : (first + count) * B, :], v_ref, block, err, slots, first, count, across)
    split_product(err, v_ref, outs[0], outs[1:])


def u_pass(first, count, across, pieces, slots, u, v, values, after):
    rows, width = count * B, u.shape[1]
    part = jax.ShapeDtypeStruct((rows // 2, width), f32)
    piece = jax.ShapeDtypeStruct((rows // 2 // pieces + PAD, width), i16)
    return pl.pallas_call(
        functools.partial(u_body, first, count, across, len(after)),
        out_shape=[part] + [piece] * pieces,
        in_specs=[SMEM, VMEM, VMEM, VMEM] + [ANY] * len(after),
        out_specs=[VMEM] * (1 + pieces),
        scratch_shapes=[pltpu.VMEM((rows, across * B), bf16)],
        compiler_params=params(),
        cost_estimate=SMALL,
        name=f"u_pass_{first}",
    )(slots, u, v, values, *after)


def sum_body(own, *refs):
    sums, at = [], 0
    for piece in refs[:-1]:
        rows = piece.shape[0] - PAD
        group = min(rows, B)
        for g in range(rows // group):
            sums.append(own[at : at + group, :] + decode(piece, g, group))
            at += group
    store_code(refs[-1], jnp.concatenate(sums, axis=0))


def core_sum(own, others):
    rows, width = own.shape
    return pl.pallas_call(
        sum_body,
        out_shape=jax.ShapeDtypeStruct((rows + PAD, width), i16),
        in_specs=[VMEM] * (1 + len(others)),
        out_specs=VMEM,
        compiler_params=params(),
        cost_estimate=SMALL,
        name="core_sum",
    )(own, *others)


def again_body(mine, mine_in, out):
    rows = mine.shape[0] - PAD
    group = min(rows, B)
    whole = [decode(mine, g, group) + decode(mine_in, g, group) for g in range(rows // group)]
    store_code(out, jnp.concatenate(whole, axis=0))


def chip_sum(code, code_in):
    return pl.pallas_call(
        again_body,
        out_shape=jax.ShapeDtypeStruct(code.shape, i16),
        in_specs=[VMEM, VMEM],
        out_specs=VMEM,
        compiler_params=params(),
        name="chip_sum",
    )(code, code_in)


def update_body(first, code, code_in, u_ref, *refs):
    out = refs[-1]
    half = out.shape[0]
    group = min(half, B)
    start = first * B + my_core() * half
    for g in range(half // group):
        old = u_ref[pl.ds(pl.multiple_of(start + g * group, 16), group), :].astype(f32)
        grad = decode(code, g, group) + decode(code_in, g, group)
        out[g * group : (g + 1) * group, :] = (old - step_u * (grad + ridge * old)).astype(bf16)


def update(first, code, code_in, u, after):
    rows, width = code.shape[0] - PAD, code.shape[1]
    return pl.pallas_call(
        functools.partial(update_body, first),
        out_shape=jax.ShapeDtypeStruct((rows, width), bf16),
        in_specs=[VMEM, VMEM, VMEM] + [ANY] * len(after),
        out_specs=VMEM,
        compiler_params=params(),
        cost_estimate=SMALL,
        name=f"update_{first}",
    )(code, code_in, u, *after)


def gather_left(left, own, others):
    mine, theirs = two_halves(left.shape[0])
    left[mine, :] = own[...]
    size = others[0].shape[0]
    for i, piece in enumerate(others):
        left[pl.ds(pl.multiple_of(theirs.start + i * size, 16), size), :] = piece[...]


def v_body(first, count, across, opening, pieces, *refs):
    slots, v_ref, values, own = refs[:4]
    others, refs = refs[4 : 4 + pieces], refs[4 + pieces :]
    if not opening:
        before = refs[0]
        refs = refs[2:]
    new_out, total, err, left, sem = refs
    gather_left(left, own, others)
    save = pltpu.make_async_copy(left, new_out.at[pl.ds(first * B, count * B)], sem)
    save.start()
    block = lambda slot, r, c: values[jnp.maximum(slot, 0)]
    residual(left[...], v_ref, block, err, slots, first, count, across)
    part = lax.dot_general(left[...], err[...], COLS_BY_COLS, preferred_element_type=f32)
    if not opening:
        part = part + before[...]
    total[...] = part
    save.wait()


def v_pass(first, count, across, slots, shape, v, values, halves, before):
    width = v.shape[1]
    times = v.shape[0]
    opening = before is None
    ins = [slots, v, values, *halves]
    in_specs = [SMEM] + [VMEM] * (2 + len(halves))
    aliases = {}
    if not opening:
        aliases = {len(ins) + 1: 0}
        ins += [before[1], before[0]]
        in_specs += [VMEM, ANY]
    return pl.pallas_call(
        functools.partial(v_body, first, count, across, opening, len(halves) - 1),
        out_shape=[jax.ShapeDtypeStruct(shape, bf16), jax.ShapeDtypeStruct((width, times), f32)],
        in_specs=in_specs,
        out_specs=[ANY, VMEM],
        input_output_aliases=aliases,
        scratch_shapes=[
            pltpu.VMEM((count * B, across * B), bf16),
            pltpu.VMEM((count * B, width), bf16),
            pltpu.SemaphoreType.DMA,
        ],
        compiler_params=params(),
        cost_estimate=SMALL,
        name=f"v_pass_{first}",
    )(*ins)


def v_end_body(first, count, across, peers, far, pieces, kinds, *refs):
    slots, v_ref, values, own = refs[:4]
    others, before, refs = refs[4 : 4 + pieces], refs[4 + pieces], refs[5 + pieces :]
    if far:
        new_out, outs = refs[1], refs[2 : 2 + len(kinds)]
    else:
        outs = refs[1 : 1 + len(kinds)]
    err, left, turned, sem = refs[-4:]
    here = lax.axis_index("svc")
    side = lax.div(here, peers // 2)
    base = (1 - side if far else side) * (across // 2)
    gather_left(left, own, others)
    if far:
        save = pltpu.make_async_copy(left, new_out.at[pl.ds(first * B, count * B)], sem)
        save.start()
    block = lambda slot, r, c: values[jnp.maximum(slot, 0)]
    residual(left[...], v_ref, block, err, slots, first, count, across, base)
    part = lax.dot_general(left[...], err[...], COLS_BY_COLS, preferred_element_type=f32)
    part = part + before[:, pl.ds(pl.multiple_of(base * B, B), across // 2 * B)]
    turned[...] = part.T
    rows = turned.shape[0] // (peers // 2)
    for (d, coded), out in zip(kinds, outs):
        there = lax.rem(jnp.bitwise_xor(here, d), peers // 2)
        part = turned[pl.ds(pl.multiple_of(there * rows, 8), rows), :]
        if coded:
            store_code(out, part)
        else:
            out[...] = part
    if far:
        save.wait()


def v_end(first, count, across, peers, far, kinds, slots, v, values, halves, before, after):
    times, width = v.shape
    rows = times // peers
    ins = [slots, v, values, *halves, before[1], after if after is not None else before[0]]
    in_specs = [SMEM] + [VMEM] * (3 + len(halves)) + [ANY]
    out = [jax.ShapeDtypeStruct((rows + PAD, width), i16) if coded else jax.ShapeDtypeStruct((rows, width), f32) for _, coded in kinds]
    out_specs = [VMEM] * len(kinds)
    if far:
        out = [jax.ShapeDtypeStruct(before[0].shape, bf16)] + out
        out_specs = [ANY] + out_specs
    return pl.pallas_call(
        functools.partial(v_end_body, first, count, across, peers, far, len(halves) - 1, kinds),
        out_shape=out,
        in_specs=in_specs,
        out_specs=out_specs,
        input_output_aliases={len(ins) - 1: 0} if far else {},
        scratch_shapes=[
            pltpu.VMEM((count * B, times // 2), bf16),
            pltpu.VMEM((count * B, width), bf16),
            pltpu.VMEM((times // 2, width), f32),
            pltpu.SemaphoreType.DMA,
        ],
        compiler_params=params(),
        cost_estimate=SMALL,
        name="v_end_far" if far else "v_end_near",
    )(*ins)


def combine_body(joined, *refs):
    outs = refs[(len(refs) + joined) // 2 :]
    owns, codes = refs[: len(outs)], refs[len(outs) : len(outs) + joined]
    for i, (own, out) in enumerate(zip(owns, outs)):
        if i < joined:
            group = min(own.shape[0], B)
            sums = [
                own[g * group : (g + 1) * group, :] + decode(codes[i], g, group)
                for g in range(own.shape[0] // group)
            ]
            store_code(out, jnp.concatenate(sums, axis=0))
        else:
            store_code(out, own[...])


def combine(owns, codes):
    rows, width = owns[0].shape
    return pl.pallas_call(
        functools.partial(combine_body, len(codes)),
        out_shape=[jax.ShapeDtypeStruct((rows + PAD, width), i16)] * len(owns),
        in_specs=[VMEM] * (len(owns) + len(codes)),
        out_specs=[VMEM] * len(owns),
        compiler_params=params(),
        cost_estimate=SMALL,
        name="combine",
    )(*owns, *codes)


def last_body(v_ref, low, high, own, *refs):
    codes, out, wide = refs[:-2], refs[-2], refs[-1]
    times = v_ref.shape[0]
    rows = out.shape[0]
    group = min(rows, B)
    wide[:PAD, :] = low[...]
    wide[PAD : PAD + times, :] = v_ref[...]
    wide[PAD + times :, :] = high[...]
    start = pl.multiple_of(lax.axis_index("svc") * rows, 16)
    window = wide[pl.ds(start, rows + 2 * PAD), :].astype(f32)
    old = window[PAD : PAD + rows]
    lap = 2.0 * old - window[PAD - 1 : PAD - 1 + rows] - window[PAD + 1 : PAD + 1 + rows]
    for g in range(rows // group):
        at = slice(g * group, (g + 1) * group)
        grad = own[at, :]
        for code in codes:
            grad = grad + decode(code, g, group)
        out[at, :] = (old[at] - step_v * (grad + ridge * old[at] + smooth * lap[at])).astype(bf16)


def last_step(v, low, high, own, codes):
    return pl.pallas_call(
        last_body,
        out_shape=jax.ShapeDtypeStruct(own.shape, bf16),
        in_specs=[VMEM] * (4 + len(codes)),
        out_specs=VMEM,
        scratch_shapes=[pltpu.VMEM((v.shape[0] + 2 * PAD, v.shape[1]), bf16)],
        compiler_params=params(),
        name="last_step",
    )(v, low, high, own, *codes)


def join_body(order, *refs):
    out = refs[-1]
    rows = refs[0].shape[0]
    for d, part in zip(order, refs[:-1]):
        there = jnp.bitwise_xor(lax.axis_index("svc"), d)
        out[pl.ds(pl.multiple_of(there * rows, 16), rows), :] = part[...]


def join(parts):
    order, parts = zip(*parts.items())
    rows, width = parts[0].shape
    return pl.pallas_call(
        functools.partial(join_body, order),
        out_shape=jax.ShapeDtypeStruct((rows * len(parts), width), bf16),
        in_specs=[VMEM] * len(parts),
        out_specs=VMEM,
        compiler_params=params(),
        cost_estimate=SMALL,
        name="join",
    )(*parts)


def swap(x, axis, mask):
    return lax.ppermute(x, axis, [(i, i ^ mask) for i in range(lax.axis_size(axis))])


def shift(x, axis, by):
    n = lax.axis_size(axis)
    return lax.ppermute(x, axis, [(i, (i + by) % n) for i in range(n)])


SHARES = (4, 6, 8, 6)


def chunks_of(down):
    unit = down // sum(SHARES)
    sizes = [unit * share for share in SHARES[:-1]]
    sizes.append(down - sum(sizes))
    return [(sum(sizes[:i]), size) for i, size in enumerate(sizes)]


def on_device(u, v, block_rows, block_cols, block_counts, block_values):
    down, across = u.shape[0] // B, v.shape[0] // B
    values = block_values[0, 0]
    steps, peers = lax.axis_size("step"), lax.axis_size("svc")
    low = shift(v[-PAD:], "step", 1)
    high = shift(v[:PAD], "step", -1)
    chunks = chunks_of(down)
    keep, send, slots = first_u_pass(chunks[0][1], down, across, (block_rows, block_cols, block_counts), u, v, values)
    codes = [core_sum(keep, [swap(send, "step", 1)])]
    arrived, halves = [], []
    before = None
    last = len(chunks) - 1

    def cross(k):
        code, mask = codes[k], 4
        code_in = swap(code, "step", 2)
        while mask < steps:
            code = chip_sum(code, code_in)
            code_in = swap(code, "step", mask)
            mask *= 2
        arrived.append((code, code_in))

    def renew(k, after):
        half = update(chunks[k][0], *arrived[k], u, after)
        pieces = 1 if k == last else pl.cdiv(chunks[k][1], chunks[k + 1][1])
        while half.shape[0] % (PAD * pieces):
            pieces += 1
        size = half.shape[0] // pieces
        halves.append((half, *(swap(half[i * size : (i + 1) * size], "step", 1) for i in range(pieces))))

    cross(0)
    token = codes[0]
    for k in range(1, last + 2):
        if k <= last:
            first, count = chunks[k]
            groups = count // 2
            pieces = min(count // chunks[k - 1][1] + 1, groups)
            while groups % pieces:
                pieces += 1
            keep, *send = u_pass(first, count, across, pieces, slots, u, v, values, [token])
            codes.append(core_sum(keep, [swap(x, "step", 1) for x in send]))
            cross(k)
        if k >= 2:
            first, count = chunks[k - 2]
            before = v_pass(first, count, across, slots, u.shape, v, values, halves[k - 2], before)
        renew(k - 1, [codes[-1]] + ([before[1]] if before else []) + ([low, high] if k > last else []))
        token = halves[k - 1][0]
    first, count = chunks[last]
    by_x = [d for d in range(peers * 3 // 4, peers) if d % 2]
    far = [(d, d + 1 not in by_x) for d in range(peers // 2, peers)]
    near = [(d, False) for d in range(peers // 2)]
    new_services, *sent = v_end(first, count, across, peers, True, far, slots, v, values, halves[last], before, None)
    sent = dict(zip((d for d, _ in far), sent))
    arrived_x = {d: swap(sent.pop(d), "svc", 1) for d in by_x}
    rest = v_end(first, count, across, peers, False, near, slots, v, values, halves[last], before, sent[peers // 2])
    own = rest[0]
    late = [d - 1 for d in by_x] + list(range(1, peers // 2))
    coded = combine([sent[d - 1] for d in by_x] + list(rest[1:]), [arrived_x[d] for d in by_x])
    sent = {d: x for d, x in sent.items() if d not in late} | dict(zip(late, coded))
    part = last_step(v, low, high, own, [swap(x, "svc", d) for d, x in sent.items()])
    column = {d: swap(part, "svc", d) for d in range(peers - 2, 0, -2)}
    column[0] = part
    for d in [x for x in column if x] + [0]:
        column[d + 1] = swap(column[d], "svc", 1)
    return new_services, join(column)


def solution(mesh):
    return jax.shard_map(
        on_device,
        mesh=mesh,
        in_specs=(
            P("svc", None),
            P("step", None),
            P("svc", "step", None),
            P("svc", "step", None),
            P("svc", "step"),
            P("svc", "step", None, None, None),
        ),
        out_specs=(P("svc", None), P("step", None)),
        check_vma=False,
    )
```

```python
import functools

import jax
import jax.numpy as jnp
from jax import lax
from jax.experimental import pallas as pl
from jax.experimental.pallas import tpu as pltpu
from jax.sharding import PartitionSpec as P

step_u = 0.03
step_v = 0.02
ridge = 0.1
smooth = 20.0

f32, bf16, i32, i16 = jnp.float32, jnp.bfloat16, jnp.int32, jnp.int16
B = 128
PAD = 16
TOP = 32000.0
ROWS_BY_ROWS = (((1,), (1,)), ((), ()))
COLS_BY_COLS = (((0,), (0,)), ((), ()))

SMEM = pl.BlockSpec(memory_space=pltpu.SMEM)
VMEM = pl.BlockSpec(memory_space=pltpu.VMEM)
ANY = pl.BlockSpec(memory_space=pl.ANY)


SMALL = pl.CostEstimate(flops=1, bytes_accessed=1, transcendentals=0)


def params():
    return pltpu.CompilerParams(vmem_limit_bytes=24 * 2**20)


def encode(x):
    rows, width = x.shape
    group = min(rows, B)
    line = lax.broadcasted_iota(i32, (PAD, width), 0)
    powers = jnp.zeros((PAD, width), f32)
    parts = []
    for g in range(rows // group):
        part = x[g * group : (g + 1) * group]
        top = jnp.max(jnp.abs(part), axis=0, keepdims=True)
        power = jnp.ceil(jnp.log2(jnp.maximum(top, 1e-30)))
        parts.append(jnp.round(part * (jnp.exp2(-power) * TOP)))
        powers = jnp.where(line == g, power, powers)
    return [p.astype(i32).astype(i16) for p in parts], powers.astype(i32).astype(i16)


def store_code(ref, x):
    parts, powers = encode(x)
    group = parts[0].shape[0]
    for g, part in enumerate(parts):
        ref[g * group : (g + 1) * group, :] = part
    ref[x.shape[0] :, :] = powers


def decode(ref, g, group):
    rows = ref.shape[0] - PAD
    powers = ref[rows:, :].astype(i32).astype(f32)[g : g + 1]
    return ref[g * group : (g + 1) * group, :].astype(i32).astype(f32) * (
        jnp.exp2(powers) * (1.0 / TOP)
    )


def my_core():
    return lax.rem(lax.axis_index("step"), 2)


def two_halves(rows):
    half = rows // 2
    core = my_core()
    return [pl.ds(pl.multiple_of(at * half, 16), half) for at in (core, 1 - core)]


def residual(left, v_ref, block, err, slots, first, count, across, base=0, ready=None):
    columns = err.shape[1] // B
    wide = min(2, columns)
    for t in range(0, columns, wide):
        start = t * B if isinstance(base, int) else pl.multiple_of((base + t) * B, B)
        predicted = lax.dot_general(
            left, v_ref[pl.ds(start, wide * B), :], ROWS_BY_ROWS, preferred_element_type=f32
        )
        if ready:
            ready(t, wide)
        for r in range(count):
            rows = slice(r * B, (r + 1) * B)
            for c in range(t, t + wide):
                slot = slots[(first + r) * across + base + c]
                gap = predicted[rows, (c - t) * B : (c - t + 1) * B] - block(slot, r, c).astype(f32)
                err[rows, c * B : (c + 1) * B] = jnp.where(slot >= 0, gap, 0.0).astype(bf16)


def split_product(err, v_ref, keep, sends):
    mine, theirs = two_halves(err.shape[0])
    whole = jnp.dot(err[theirs, :], v_ref[...], preferred_element_type=f32)
    size = whole.shape[0] // len(sends)
    for i, send in enumerate(sends):
        store_code(send, whole[i * size : (i + 1) * size])
    keep[...] = jnp.dot(err[mine, :], v_ref[...], preferred_element_type=f32)


def first_u_body(
    count, down, across, row_hbm, col_hbm, live_ref, u_hbm, v_hbm, values,
    keep, send, slots, row_ref, col_ref, dense, err, left, v_ref, sems
):
    loads = [
        pltpu.make_async_copy(src, dst, sems.at[i])
        for i, (src, dst) in enumerate(
            (
                (row_hbm, row_ref),
                (col_hbm, col_ref),
                (u_hbm.at[pl.ds(0, count * B)], left),
                (v_hbm, v_ref),
            )
        )
    ]
    for load in loads:
        load.start()

    def clear(i, c):
        slots[i] = jnp.int32(-1)
        return c

    lax.fori_loop(0, down * across, clear, 0, unroll=8)
    for load in loads[:2]:
        load.wait()
    live = live_ref[0, 0]

    total = row_ref.shape[2]
    batch = next(n for n in (14, 11, 8, 7, 4, 2, 1) if total % n == 0)

    def enter(i, c):
        at = [i * batch + j for j in range(batch)]
        where = [row_ref[0, 0, k] * across + col_ref[0, 0, k] for k in at]
        for k, place in zip(at, where):
            slots[place] = jnp.where(k < live, k, -1)
        return c

    lax.fori_loop(0, total // batch, enter, 0)
    sem = sems.at[len(loads)]

    def fetch(c):
        def go(r, started):
            slot = slots[r * across + c]

            @pl.when(slot >= 0)
            def _():
                row = pl.multiple_of(r * B, B)
                pltpu.make_async_copy(values.at[slot], dense.at[c, pl.ds(row, B)], sem).start()

            return started + (slot >= 0).astype(i32)

        return lax.fori_loop(0, count, go, jnp.int32(0), unroll=True)

    started = sum(fetch(c) for c in range(across))
    for load in loads[2:]:
        load.wait()

    def wait(_, c):
        pltpu.make_async_copy(values.at[0], dense.at[0, pl.ds(0, B)], sem).wait()
        return c

    def ready(t, wide):
        if t == 0:
            lax.fori_loop(0, started, wait, 0)

    block = lambda slot, r, c: dense[c, r * B : (r + 1) * B, :]
    residual(left[...], v_ref, block, err, slots, 0, count, across, 0, ready)
    split_product(err, v_ref, keep, [send])


def in_hbm(x):
    return pltpu.with_memory_space_constraint(x, pltpu.HBM)


def first_u_pass(count, down, across, index, u, v, values):
    rows, width = count * B, u.shape[1]
    hbm = pl.BlockSpec(memory_space=pltpu.HBM)
    part = jax.ShapeDtypeStruct((rows // 2, width), f32)
    return pl.pallas_call(
        functools.partial(first_u_body, count, down, across),
        out_shape=[part, jax.ShapeDtypeStruct((rows // 2 + PAD, width), i16), jax.ShapeDtypeStruct((down * across,), i32)],
        in_specs=[hbm, hbm, SMEM, hbm, hbm, hbm],
        out_specs=[VMEM, VMEM, SMEM],
        scratch_shapes=[
            *(pltpu.SMEM(x.shape, i32) for x in index[:2]),
            pltpu.VMEM((across, rows, B), bf16),
            pltpu.VMEM((rows, across * B), bf16),
            pltpu.VMEM((rows, width), bf16),
            pltpu.VMEM(v.shape, bf16),
            pltpu.SemaphoreType.DMA((5,)),
        ],
        compiler_params=params(),
        cost_estimate=SMALL,
        name="u_pass_0",
    )(*(in_hbm(x) for x in index[:2]), index[2], *(in_hbm(x) for x in (u, v, values)))


def u_body(first, count, across, waits, slots, u_ref, v_ref, values, *refs):
    outs, err = refs[waits:-1], refs[-1]
    block = lambda slot, r, c: values[jnp.maximum(slot, 0)]
    residual(u_ref[first * B : (first + count) * B, :], v_ref, block, err, slots, first, count, across)
    split_product(err, v_ref, outs[0], outs[1:])


def u_pass(first, count, across, pieces, slots, u, v, values, after):
    rows, width = count * B, u.shape[1]
    part = jax.ShapeDtypeStruct((rows // 2, width), f32)
    piece = jax.ShapeDtypeStruct((rows // 2 // pieces + PAD, width), i16)
    return pl.pallas_call(
        functools.partial(u_body, first, count, across, len(after)),
        out_shape=[part] + [piece] * pieces,
        in_specs=[SMEM, VMEM, VMEM, VMEM] + [ANY] * len(after),
        out_specs=[VMEM] * (1 + pieces),
        scratch_shapes=[pltpu.VMEM((rows, across * B), bf16)],
        compiler_params=params(),
        cost_estimate=SMALL,
        name=f"u_pass_{first}",
    )(slots, u, v, values, *after)


def sum_body(own, *refs):
    sums, at = [], 0
    for piece in refs[:-1]:
        rows = piece.shape[0] - PAD
        group = min(rows, B)
        for g in range(rows // group):
            sums.append(own[at : at + group, :] + decode(piece, g, group))
            at += group
    store_code(refs[-1], jnp.concatenate(sums, axis=0))


def core_sum(own, others):
    rows, width = own.shape
    return pl.pallas_call(
        sum_body,
        out_shape=jax.ShapeDtypeStruct((rows + PAD, width), i16),
        in_specs=[VMEM] * (1 + len(others)),
        out_specs=VMEM,
        compiler_params=params(),
        cost_estimate=SMALL,
        name="core_sum",
    )(own, *others)


def again_body(mine, mine_in, out):
    rows = mine.shape[0] - PAD
    group = min(rows, B)
    whole = [decode(mine, g, group) + decode(mine_in, g, group) for g in range(rows // group)]
    store_code(out, jnp.concatenate(whole, axis=0))


def chip_sum(code, code_in):
    return pl.pallas_call(
        again_body,
        out_shape=jax.ShapeDtypeStruct(code.shape, i16),
        in_specs=[VMEM, VMEM],
        out_specs=VMEM,
        compiler_params=params(),
        name="chip_sum",
    )(code, code_in)


def update_body(first, code, code_in, u_ref, *refs):
    out = refs[-1]
    half = out.shape[0]
    group = min(half, B)
    start = first * B + my_core() * half
    for g in range(half // group):
        old = u_ref[pl.ds(pl.multiple_of(start + g * group, 16), group), :].astype(f32)
        grad = decode(code, g, group) + decode(code_in, g, group)
        out[g * group : (g + 1) * group, :] = (old - step_u * (grad + ridge * old)).astype(bf16)


def update(first, code, code_in, u, after):
    rows, width = code.shape[0] - PAD, code.shape[1]
    return pl.pallas_call(
        functools.partial(update_body, first),
        out_shape=jax.ShapeDtypeStruct((rows, width), bf16),
        in_specs=[VMEM, VMEM, VMEM] + [ANY] * len(after),
        out_specs=VMEM,
        compiler_params=params(),
        cost_estimate=SMALL,
        name=f"update_{first}",
    )(code, code_in, u, *after)


def gather_left(left, own, others):
    mine, theirs = two_halves(left.shape[0])
    left[mine, :] = own[...]
    size = others[0].shape[0]
    for i, piece in enumerate(others):
        left[pl.ds(pl.multiple_of(theirs.start + i * size, 16), size), :] = piece[...]


def v_body(first, count, across, opening, pieces, *refs):
    slots, v_ref, values, own = refs[:4]
    others, refs = refs[4 : 4 + pieces], refs[4 + pieces :]
    if not opening:
        before = refs[0]
        refs = refs[2:]
    new_out, total, err, left, sem = refs
    gather_left(left, own, others)
    save = pltpu.make_async_copy(left, new_out.at[pl.ds(first * B, count * B)], sem)
    save.start()
    block = lambda slot, r, c: values[jnp.maximum(slot, 0)]
    residual(left[...], v_ref, block, err, slots, first, count, across)
    part = lax.dot_general(left[...], err[...], COLS_BY_COLS, preferred_element_type=f32)
    if not opening:
        part = part + before[...]
    total[...] = part
    save.wait()


def v_pass(first, count, across, slots, shape, v, values, halves, before):
    width = v.shape[1]
    times = v.shape[0]
    opening = before is None
    ins = [slots, v, values, *halves]
    in_specs = [SMEM] + [VMEM] * (2 + len(halves))
    aliases = {}
    if not opening:
        aliases = {len(ins) + 1: 0}
        ins += [before[1], before[0]]
        in_specs += [VMEM, ANY]
    return pl.pallas_call(
        functools.partial(v_body, first, count, across, opening, len(halves) - 1),
        out_shape=[jax.ShapeDtypeStruct(shape, bf16), jax.ShapeDtypeStruct((width, times), f32)],
        in_specs=in_specs,
        out_specs=[ANY, VMEM],
        input_output_aliases=aliases,
        scratch_shapes=[
            pltpu.VMEM((count * B, across * B), bf16),
            pltpu.VMEM((count * B, width), bf16),
            pltpu.SemaphoreType.DMA,
        ],
        compiler_params=params(),
        cost_estimate=SMALL,
        name=f"v_pass_{first}",
    )(*ins)


def v_end_body(first, count, across, peers, far, pieces, kinds, *refs):
    slots, v_ref, values, own = refs[:4]
    others, before, refs = refs[4 : 4 + pieces], refs[4 + pieces], refs[5 + pieces :]
    if far:
        new_out, outs = refs[1], refs[2 : 2 + len(kinds)]
    else:
        outs = refs[1 : 1 + len(kinds)]
    err, left, turned, sem = refs[-4:]
    here = lax.axis_index("svc")
    side = lax.div(here, peers // 2)
    base = (1 - side if far else side) * (across // 2)
    gather_left(left, own, others)
    if far:
        save = pltpu.make_async_copy(left, new_out.at[pl.ds(first * B, count * B)], sem)
        save.start()
    block = lambda slot, r, c: values[jnp.maximum(slot, 0)]
    residual(left[...], v_ref, block, err, slots, first, count, across, base)
    part = lax.dot_general(left[...], err[...], COLS_BY_COLS, preferred_element_type=f32)
    part = part + before[:, pl.ds(pl.multiple_of(base * B, B), across // 2 * B)]
    turned[...] = part.T
    rows = turned.shape[0] // (peers // 2)
    for (d, coded), out in zip(kinds, outs):
        there = lax.rem(jnp.bitwise_xor(here, d), peers // 2)
        part = turned[pl.ds(pl.multiple_of(there * rows, 8), rows), :]
        if coded:
            store_code(out, part)
        else:
            out[...] = part
    if far:
        save.wait()


def v_end(first, count, across, peers, far, kinds, slots, v, values, halves, before, after):
    times, width = v.shape
    rows = times // peers
    ins = [slots, v, values, *halves, before[1], after if after is not None else before[0]]
    in_specs = [SMEM] + [VMEM] * (3 + len(halves)) + [ANY]
    out = [jax.ShapeDtypeStruct((rows + PAD, width), i16) if coded else jax.ShapeDtypeStruct((rows, width), f32) for _, coded in kinds]
    out_specs = [VMEM] * len(kinds)
    if far:
        out = [jax.ShapeDtypeStruct(before[0].shape, bf16)] + out
        out_specs = [ANY] + out_specs
    return pl.pallas_call(
        functools.partial(v_end_body, first, count, across, peers, far, len(halves) - 1, kinds),
        out_shape=out,
        in_specs=in_specs,
        out_specs=out_specs,
        input_output_aliases={len(ins) - 1: 0} if far else {},
        scratch_shapes=[
            pltpu.VMEM((count * B, times // 2), bf16),
            pltpu.VMEM((count * B, width), bf16),
            pltpu.VMEM((times // 2, width), f32),
            pltpu.SemaphoreType.DMA,
        ],
        compiler_params=params(),
        cost_estimate=SMALL,
        name="v_end_far" if far else "v_end_near",
    )(*ins)


def combine_body(joined, *refs):
    outs = refs[(len(refs) + joined) // 2 :]
    owns, codes = refs[: len(outs)], refs[len(outs) : len(outs) + joined]
    for i, (own, out) in enumerate(zip(owns, outs)):
        if i < joined:
            group = min(own.shape[0], B)
            sums = [
                own[g * group : (g + 1) * group, :] + decode(codes[i], g, group)
                for g in range(own.shape[0] // group)
            ]
            store_code(out, jnp.concatenate(sums, axis=0))
        else:
            store_code(out, own[...])


def combine(owns, codes):
    rows, width = owns[0].shape
    return pl.pallas_call(
        functools.partial(combine_body, len(codes)),
        out_shape=[jax.ShapeDtypeStruct((rows + PAD, width), i16)] * len(owns),
        in_specs=[VMEM] * (len(owns) + len(codes)),
        out_specs=[VMEM] * len(owns),
        compiler_params=params(),
        cost_estimate=SMALL,
        name="combine",
    )(*owns, *codes)


def last_body(v_ref, low, high, own, *refs):
    codes, out, wide = refs[:-2], refs[-2], refs[-1]
    times = v_ref.shape[0]
    rows = out.shape[0]
    group = min(rows, B)
    wide[:PAD, :] = low[...]
    wide[PAD : PAD + times, :] = v_ref[...]
    wide[PAD + times :, :] = high[...]
    start = pl.multiple_of(lax.axis_index("svc") * rows, 16)
    window = wide[pl.ds(start, rows + 2 * PAD), :].astype(f32)
    old = window[PAD : PAD + rows]
    lap = 2.0 * old - window[PAD - 1 : PAD - 1 + rows] - window[PAD + 1 : PAD + 1 + rows]
    for g in range(rows // group):
        at = slice(g * group, (g + 1) * group)
        grad = own[at, :]
        for code in codes:
            grad = grad + decode(code, g, group)
        out[at, :] = (old[at] - step_v * (grad + ridge * old[at] + smooth * lap[at])).astype(bf16)


def last_step(v, low, high, own, codes):
    return pl.pallas_call(
        last_body,
        out_shape=jax.ShapeDtypeStruct(own.shape, bf16),
        in_specs=[VMEM] * (4 + len(codes)),
        out_specs=VMEM,
        scratch_shapes=[pltpu.VMEM((v.shape[0] + 2 * PAD, v.shape[1]), bf16)],
        compiler_params=params(),
        name="last_step",
    )(v, low, high, own, *codes)


def join_body(order, *refs):
    out = refs[-1]
    rows = refs[0].shape[0]
    for d, part in zip(order, refs[:-1]):
        there = jnp.bitwise_xor(lax.axis_index("svc"), d)
        out[pl.ds(pl.multiple_of(there * rows, 16), rows), :] = part[...]


def join(parts):
    order, parts = zip(*parts.items())
    rows, width = parts[0].shape
    return pl.pallas_call(
        functools.partial(join_body, order),
        out_shape=jax.ShapeDtypeStruct((rows * len(parts), width), bf16),
        in_specs=[VMEM] * len(parts),
        out_specs=VMEM,
        compiler_params=params(),
        cost_estimate=SMALL,
        name="join",
    )(*parts)


def swap(x, axis, mask):
    return lax.ppermute(x, axis, [(i, i ^ mask) for i in range(lax.axis_size(axis))])


def shift(x, axis, by):
    n = lax.axis_size(axis)
    return lax.ppermute(x, axis, [(i, (i + by) % n) for i in range(n)])


SHARES = (4, 6, 8, 6)


def chunks_of(down):
    unit = down // sum(SHARES)
    sizes = [unit * share for share in SHARES[:-1]]
    sizes.append(down - sum(sizes))
    return [(sum(sizes[:i]), size) for i, size in enumerate(sizes)]


def on_device(u, v, block_rows, block_cols, block_counts, block_values):
    down, across = u.shape[0] // B, v.shape[0] // B
    values = block_values[0, 0]
    steps, peers = lax.axis_size("step"), lax.axis_size("svc")
    low = shift(v[-PAD:], "step", 1)
    high = shift(v[:PAD], "step", -1)
    chunks = chunks_of(down)
    keep, send, slots = first_u_pass(chunks[0][1], down, across, (block_rows, block_cols, block_counts), u, v, values)
    codes = [core_sum(keep, [swap(send, "step", 1)])]
    arrived, halves = [], []
    before = None
    last = len(chunks) - 1

    def cross(k):
        code, mask = codes[k], 4
        code_in = swap(code, "step", 2)
        while mask < steps:
            code = chip_sum(code, code_in)
            code_in = swap(code, "step", mask)
            mask *= 2
        arrived.append((code, code_in))

    def renew(k, after):
        half = update(chunks[k][0], *arrived[k], u, after)
        pieces = 1 if k == last else pl.cdiv(chunks[k][1], chunks[k + 1][1])
        while half.shape[0] % (PAD * pieces):
            pieces += 1
        size = half.shape[0] // pieces
        halves.append((half, *(swap(half[i * size : (i + 1) * size], "step", 1) for i in range(pieces))))

    cross(0)
    token = codes[0]
    for k in range(1, last + 2):
        if k <= last:
            first, count = chunks[k]
            groups = count // 2
            pieces = min(count // chunks[k - 1][1] + 1, groups)
            while groups % pieces:
                pieces += 1
            keep, *send = u_pass(first, count, across, pieces, slots, u, v, values, [token])
            codes.append(core_sum(keep, [swap(x, "step", 1) for x in send]))
            cross(k)
        if k >= 2:
            first, count = chunks[k - 2]
            before = v_pass(first, count, across, slots, u.shape, v, values, halves[k - 2], before)
        renew(k - 1, [codes[-1]] + ([before[1]] if before else []) + ([low, high] if k > last else []))
        token = halves[k - 1][0]
    first, count = chunks[last]
    by_x = [d for d in range(peers * 3 // 4, peers) if d % 2]
    far = [(d, d + 1 not in by_x) for d in range(peers // 2, peers)]
    near = [(d, False) for d in range(peers // 2)]
    new_services, *sent = v_end(first, count, across, peers, True, far, slots, v, values, halves[last], before, None)
    sent = dict(zip((d for d, _ in far), sent))
    arrived_x = {d: swap(sent.pop(d), "svc", 1) for d in by_x}
    rest = v_end(first, count, across, peers, False, near, slots, v, values, halves[last], before, sent[peers // 2])
    own = rest[0]
    late = [d - 1 for d in by_x] + list(range(1, peers // 2))
    coded = combine([sent[d - 1] for d in by_x] + list(rest[1:]), [arrived_x[d] for d in by_x])
    coded = dict(zip(late, coded))
    sent = {d: x for d, x in sent.items() if d not in late} | {d: coded[d] for d in sorted(late)}
    part = last_step(v, low, high, own, [swap(x, "svc", d) for d, x in sent.items()])
    column = {d: swap(part, "svc", d) for d in range(peers - 2, 0, -2)}
    column[0] = part
    for d in [x for x in column if x] + [0]:
        column[d + 1] = swap(column[d], "svc", 1)
    return new_services, join(column)


def solution(mesh):
    return jax.shard_map(
        on_device,
        mesh=mesh,
        in_specs=(
            P("svc", None),
            P("step", None),
            P("svc", "step", None),
            P("svc", "step", None),
            P("svc", "step"),
            P("svc", "step", None, None, None),
        ),
        out_specs=(P("svc", None), P("step", None)),
        check_vma=False,
    )
```
